32 devices in a mesh: gx: 8 (over z, y), gy: 4 (over x, core).
Axes of the slice: x: 2, y: 2, z: 4, core: 2. Of those that a mesh axis runs over, the one named last changes fastest.
Arguments:
- populations: float32 [27, 64, 128, 128], P(None, 'gx', 'gy'), may hold values from 0.49 to 1.69
- precursor: float32 [27, 16, 128, 128], P(None, 'gx', 'gy'), may hold values from 0.49 to 1.69
- pairing: int32 [8], replicated, may hold values from 0 to 7, each once
- rates: float32 [27], replicated, may hold values from 0.5 to 1.9
- loading: float32 [32], replicated, may hold values from 4 to 32
- disc_cols: int32 [512], replicated, may hold values from 0 to 8191, as said below
- disc_turb: int32 [512], replicated, may hold values from -1 to 31, as said below
Outputs:
- read: float32 [27, 64, 128, 128], P(None, 'gx', 'gy')
- disc_speed: float32 [32], replicated
The draws below stay inside these ranges and needn't reach their ends.
Inputs may be any that keep to these rules, and one draw needn't show every extreme that they name: `disc_cols`: each turbine's used slots name 8 to 16 spanwise-adjacent columns (periodic in y) of one streamwise plane; unused slots hold column 0. `disc_turb`: every turbine id 0..31 has 8 to 16 used slots, both counts reached; -1 marks an unused slot; slots are in no particular order.
All inputs are finite; a program needn't handle non-finite values.
Results may differ from the reference program's by a relative error of at most 0.00009.
Values sent between devices are 32-bit elements; how exact they have to be, the bound alone decides.
A program may use at most 128 MiB of HBM per device.

```python
import math
import jax
import jax.numpy as jnp
import numpy as np
from jax import lax

CX = 8
FR = 2
NT = 32
DMAX = 16
NX = 64
NY = 128
NZ = 128
FRX = 16
NR = 512
N_GX = 8


def flow_factor():
    steps = (jnp.arange(27, dtype=jnp.int32) // 9 - 1).astype(jnp.float32)
    return (1.0 + 0.3 * steps).reshape(27, 1, 1, 1)


def draw_populations(key, part):
    shape = (27, NX, NY, NZ)
    noise = jax.random.uniform(key, shape, jnp.float32, -0.3, 0.3)
    return flow_factor() * (1.0 + noise)


def draw_precursor(key, part):
    shape = (27, FRX, NY, NZ)
    inner = jax.random.fold_in(key, 5)
    noise = jax.random.uniform(inner, shape, jnp.float32, -0.3, 0.3)
    return flow_factor() * (1.0 + noise)


def disc_layout(key):
    inner = jax.random.fold_in(key, 11)
    key_a, key_b, key_c, key_d = jax.random.split(inner, 4)
    planes = jax.random.randint(key_a, (NT,), 0, NX)
    centres = jax.random.randint(key_b, (NT,), 0, NY)
    spans = jax.random.randint(key_c, (NT,), DMAX // 2, DMAX + 1)
    spans = spans.at[0].set(DMAX // 2).at[1].set(DMAX)
    slots = jnp.arange(NR, dtype=jnp.int32)
    owner = slots // DMAX
    offset = slots % DMAX
    used = offset < spans[owner]
    column = planes[owner] * NY + (centres[owner] - spans[owner] // 2 + offset) % NY
    turbine = jnp.where(used, owner, -1)
    column = jnp.where(used, column, 0)
    order = jax.random.permutation(key_d, NR)
    return (column[order].astype(jnp.int32), turbine[order].astype(jnp.int32))


def draw_disc_cols(key, part):
    return disc_layout(key)[0]


def draw_disc_turb(key, part):
    return disc_layout(key)[1]


def setup_inputs(seed: int = 0) -> dict:
    key_list = jax.random.split(jax.random.key(seed), 8)
    populations = draw_populations(jax.random.fold_in(key_list[7], 71), 0)
    precursor = draw_precursor(jax.random.fold_in(key_list[7], 71), 0)
    pairing = jax.random.permutation(key_list[2], N_GX).astype(jnp.int32)
    rates = jnp.clip(jnp.exp(jax.random.uniform(key_list[3], (27,), jnp.float32, math.log(0.5), math.log(1.9))), 0.5, 1.9)
    loading = jnp.clip(jnp.exp(jax.random.uniform(key_list[4], (NT,), jnp.float32, math.log(4.0), math.log(32.0))), 4.0, 32.0)
    disc_cols = draw_disc_cols(jax.random.fold_in(key_list[7], 71), 0)
    disc_turb = draw_disc_turb(jax.random.fold_in(key_list[7], 71), 0)
    return {"populations": populations, "precursor": precursor, "pairing": pairing, "rates": rates, "loading": loading, "disc_cols": disc_cols, "disc_turb": disc_turb}


FULL_PRECISION = lax.Precision.HIGHEST


def lattice_tables():
    steps_one = np.array([-1.0, 0.0, 1.0])
    weight_one = np.array([1.0 / 6.0, 2.0 / 3.0, 1.0 / 6.0])
    grid_x, grid_y, grid_z = np.meshgrid(np.arange(3), np.arange(3), np.arange(3), indexing="ij")
    grid_x = grid_x.ravel()
    grid_y = grid_y.ravel()
    grid_z = grid_z.ravel()
    shift_x = steps_one[grid_x]
    shift_y = steps_one[grid_y]
    shift_z = steps_one[grid_z]
    weights = weight_one[grid_x] * weight_one[grid_y] * weight_one[grid_z]
    vander = np.array([[1.0, 1.0, 1.0], [-1.0, 0.0, 1.0], [1.0, 0.0, 1.0]])
    inverse = np.array([[0.0, -0.5, 0.5], [1.0, 0.0, -1.0], [0.0, 0.5, 0.5]])
    moment_map = np.kron(np.kron(vander, vander), vander) * weights[None, :]
    back_map = np.kron(np.kron(inverse, inverse), inverse) / weights[:, None]
    third = 1.0 / 3.0
    fringe_map = np.stack([weights, weights * shift_x, weights * shift_y, weights * shift_z,
                           weights * shift_x * shift_x, weights * shift_y * shift_y, weights * shift_z * shift_z,
                           weights * shift_x * shift_y, weights * shift_x * shift_z, weights * shift_y * shift_z])
    quad_x = shift_x * shift_x - third
    quad_y = shift_y * shift_y - third
    quad_z = shift_z * shift_z - third
    rebuild_map = np.stack([1.0 - 1.5 * (quad_x + quad_y + quad_z), 3.0 * shift_x, 3.0 * shift_y, 3.0 * shift_z,
                            4.5 * quad_x, 4.5 * quad_y, 4.5 * quad_z,
                            9.0 * shift_x * shift_y, 9.0 * shift_x * shift_z, 9.0 * shift_y * shift_z], axis=1)
    tables = (shift_x, shift_y, shift_z, moment_map, back_map, fringe_map, rebuild_map)
    return tuple(jnp.asarray(table, dtype=jnp.float32) for table in tables)


def disc_profile(depth):
    heights = jnp.arange(depth).astype(jnp.float32)
    return jnp.exp(-jnp.square((heights - depth / 3.0) / (depth / 6.0)))


def relax_cells(tables, moments, rates, force):
    shift_x, shift_y, shift_z, moment_map, back_map = tables[:5]
    density = moments[0]
    velocity_x = moments[9] / density
    velocity_y = moments[3] / density
    velocity_z = moments[1] / density
    projected = shift_x[:, None] * velocity_x[None, :] + shift_y[:, None] * velocity_y[None, :] + shift_z[:, None] * velocity_z[None, :]
    speed_sq = velocity_x * velocity_x + velocity_y * velocity_y + velocity_z * velocity_z
    balance = density[None, :] * (1.0 + 3.0 * projected + 4.5 * projected * projected - 1.5 * speed_sq[None, :])
    balance_moments = jnp.dot(moment_map, balance, precision=FULL_PRECISION)
    relaxed = moments - rates[:, None] * (moments - balance_moments)
    return jnp.dot(back_map, relaxed, precision=FULL_PRECISION) + 3.0 * shift_x[:, None] * force[None, :]


def reference(populations, precursor, pairing, rates, loading, disc_cols, disc_turb):
    tables = lattice_tables()
    flat = populations.reshape(27, NX * NY * NZ)
    moments = jnp.dot(tables[3], flat, precision=FULL_PRECISION)
    velocity_x = moments[9] / moments[0]
    profile = disc_profile(NZ)
    columns = velocity_x.reshape(NX * NY, NZ)[disc_cols]
    row_values = jnp.dot(columns, profile, precision=FULL_PRECISION)
    owner_table = (disc_turb[None, :] == jnp.arange(NT, dtype=jnp.int32)[:, None]).astype(jnp.float32)
    totals = jnp.dot(owner_table, row_values, precision=FULL_PRECISION)
    counts = jnp.sum(owner_table, axis=1)
    disc_speed = totals / (counts * jnp.sum(profile))
    thrust = 0.5 * loading * disc_speed * jnp.abs(disc_speed)
    row_thrust = jnp.dot(thrust, owner_table, precision=FULL_PRECISION)
    column_force = jnp.zeros((NX * NY,), jnp.float32).at[disc_cols].add(row_thrust)
    force = -(column_force[:, None] * profile[None, :]).reshape(NX * NY * NZ)
    post = relax_cells(tables, moments, rates, force).reshape(27, NX, NY, NZ)
    reduced = jnp.dot(tables[5], precursor.reshape(27, FRX * NY * NZ), precision=FULL_PRECISION)
    rebuilt = jnp.dot(tables[6], reduced, precision=FULL_PRECISION).reshape(27, FRX, NY, NZ)
    planes = jnp.arange(FR, dtype=jnp.int32)
    targets = (jnp.arange(N_GX, dtype=jnp.int32)[:, None] * CX + planes[None, :]).reshape(-1)
    sources = (pairing[:, None] * FR + planes[None, :]).reshape(-1)
    blend = jnp.tile(0.5 / (planes.astype(jnp.float32) + 1.0), N_GX)[None, :, None, None]
    mixed = (1.0 - blend) * post[:, targets] + blend * rebuilt[:, sources]
    post = post.at[:, targets].set(mixed)
    pieces = []
    for slot in range(27):
        step_x = slot // 9 - 1
        step_y = (slot // 3) % 3 - 1
        step_z = slot % 3 - 1
        moved = jnp.roll(post[slot], (step_x, step_y), axis=(0, 1))
        if step_z == 1:
            moved = jnp.concatenate([post[26 - slot][:, :, :1], moved[:, :, :-1]], axis=2)
        elif step_z == -1:
            moved = jnp.concatenate([moved[:, :, 1:], post[26 - slot][:, :, -1:]], axis=2)
        pieces.append(moved)
    return jnp.stack(pieces), disc_speed
```

```python
import functools
import jax
import jax.numpy as jnp
import numpy as np
from jax import lax
from jax.experimental import pallas as pl
from jax.experimental.pallas import tpu as pltpu
from jax.sharding import PartitionSpec as P

MESH = pl.DeviceIdType.MESH
LANES = 128
BLOCK = 8
LOW = (0, 9, 3, 1, 18, 6, 2, 12, 10, 4)


def forward(cells):
    cells = list(cells)
    for stride in (9, 3, 1):
        for i in range(27):
            if (i // stride) % 3 == 0:
                low, mid, high = cells[i], cells[i + stride], cells[i + 2 * stride]
                even = (low + high) * (1.0 / 6.0)
                cells[i] = even + mid * (2.0 / 3.0)
                cells[i + stride] = (high - low) * (1.0 / 6.0)
                cells[i + 2 * stride] = even
    return cells


def backward(moments):
    cells = list(moments)
    for stride in (9, 3, 1):
        for i in range(27):
            if (i // stride) % 3 == 0:
                zero, one, two = cells[i], cells[i + stride], cells[i + 2 * stride]
                odd, even = one * 3.0, two * 3.0
                cells[i] = even - odd
                cells[i + stride] = (zero - two) * 1.5
                cells[i + 2 * stride] = even + odd
    return cells


def balance_moments(density, velocity):
    flux = [density * v for v in velocity]
    out = []
    for i in range(27):
        powers = (i // 9, (i // 3) % 3, i % 3)
        scale = (1.0 / 3.0) ** sum(p == 2 for p in powers)
        odd = [d for d in range(3) if powers[d] == 1]
        if len(odd) == 3:
            out.append(None)
            continue
        if len(odd) == 2:
            value = flux[odd[0]] * velocity[odd[1]]
        elif len(odd) == 1:
            value = flux[odd[0]]
        else:
            value = density
            for d in range(3):
                if powers[d] == 2:
                    value = value + 3.0 * (flux[d] * velocity[d])
        out.append(value if scale == 1.0 else value * scale)
    return out


def rebuild(low):
    rho, jx, jy, jz, xx, yy, zz, xy, xz, yz = low
    base = 2.5 * rho - 1.5 * (xx + yy + zz)
    third = rho * (1.0 / 3.0)
    linear = (3.0 * jx, 3.0 * jy, 3.0 * jz)
    square = (4.5 * (xx - third), 4.5 * (yy - third), 4.5 * (zz - third))
    cross = (9.0 * xy, 9.0 * xz, 9.0 * yz)

    def one(d, step):
        return square[d] + linear[d] if step > 0 else square[d] - linear[d]

    def signed(value, term, sign):
        return value + term if sign > 0 else value - term

    out = []
    for i in range(27):
        steps = (i // 9 - 1, (i // 3) % 3 - 1, i % 3 - 1)
        value = base
        for d in range(3):
            if steps[d]:
                value = value + one(d, steps[d])
        for (a, b), term in zip(((0, 1), (0, 2), (1, 2)), cross):
            if steps[a] * steps[b]:
                value = signed(value, term, steps[a] * steps[b])
        out.append(value)
    return out


def row_of(kx, kz):
    return kx * 3 + kz if kx < 2 else 8 + kz


def kernel(
    n, m, chunk,
    pops_hbm, prec_hbm, pairing, rates, loading, cols, turb,
    out_hbm, speed,
    pops, prec, post, outv, mom, got, stage, final, tot_x, tot_y, load_pad, hits, ysend, yrecv,
    in_sem, out_sem, a_send, a_recv, b_send, b_recv, tx_send, tx_recv, ty_send, ty_recv,
    x_send, x_recv, y_send, y_recv, c_send, c_recv,
):
    comps, width_x, width_y, depth = pops.shape
    fringe = prec.shape[1]
    turbines = loading.shape[1]
    blocks = width_y // BLOCK
    me, my = lax.axis_index("gx"), lax.axis_index("gy")
    right, left = lax.rem(me + 1, n), lax.rem(me + n - 1, n)
    above, below = lax.rem(my + 1, m), lax.rem(my + m - 1, m)

    prec_in = pltpu.make_async_copy(prec_hbm, prec, in_sem.at[0])
    pops_in = pltpu.make_async_copy(pops_hbm, pops, in_sem.at[1])
    prec_in.start()
    pops_in.start()

    barrier = pltpu.get_barrier_semaphore()

    def greet_x(i, _):
        pl.semaphore_signal(barrier, inc=1, device_id={"gx": lax.rem(me + i, n)}, device_id_type=MESH)
        return 0

    def greet_y(i, _):
        pl.semaphore_signal(barrier, inc=1, device_id={"gy": lax.rem(my + i, m)}, device_id_type=MESH)
        return 0

    lax.fori_loop(1, n, greet_x, 0)
    lax.fori_loop(1, m, greet_y, 0)

    heights = lax.broadcasted_iota(jnp.int32, (BLOCK, depth), 1).astype(jnp.float32)
    profile = jnp.exp(-jnp.square((heights - depth / 3.0) / (depth / 6.0)))

    prec_in.wait()
    for p in range(fringe):
        def precursor_block(b, _, p=p):
            rows = pl.ds(pl.multiple_of(b * BLOCK, BLOCK), BLOCK)
            moments = forward([prec[i, p, rows, :] for i in range(27)])
            for q in range(10):
                start = pl.multiple_of((p * 10 + q) * width_y + b * BLOCK, BLOCK)
                mom[pl.ds(start, BLOCK), :] = moments[LOW[q]]
            return 0

        lax.fori_loop(0, blocks, precursor_block, 0)

    pl.semaphore_wait(barrier, n + m - 2)

    def span(j):
        return pl.ds(pl.multiple_of(j * chunk, BLOCK), chunk)

    def first(i):
        to = lax.rem(me + i, n)
        return pltpu.make_async_remote_copy(
            src_ref=mom.at[span(to), :], dst_ref=got.at[me],
            send_sem=a_send.at[to], recv_sem=a_recv.at[me],
            device_id={"gx": to}, device_id_type=MESH)

    def first_in(i):
        source = lax.rem(me + i, n)
        return pltpu.make_async_remote_copy(
            src_ref=mom.at[span(source), :], dst_ref=got.at[source],
            send_sem=a_send.at[source], recv_sem=a_recv.at[source],
            device_id={"gx": source}, device_id_type=MESH)

    def second(i):
        to = lax.rem(me + i, n)
        return pltpu.make_async_remote_copy(
            src_ref=stage.at[to], dst_ref=final.at[span(me), :],
            send_sem=b_send.at[to], recv_sem=b_recv.at[me],
            device_id={"gx": to}, device_id_type=MESH)

    def second_in(i):
        source = lax.rem(me + i, n)
        return pltpu.make_async_remote_copy(
            src_ref=stage.at[source], dst_ref=final.at[span(source), :],
            send_sem=b_send.at[source], recv_sem=b_recv.at[source],
            device_id={"gx": source}, device_id_type=MESH)

    def total_x(i):
        to = lax.rem(me + i, n)
        return pltpu.make_async_remote_copy(
            src_ref=tot_x.at[me], dst_ref=tot_x.at[me],
            send_sem=tx_send.at[to], recv_sem=tx_recv.at[me],
            device_id={"gx": to}, device_id_type=MESH)

    def total_x_in(i):
        source = lax.rem(me + i, n)
        return pltpu.make_async_remote_copy(
            src_ref=tot_x.at[source], dst_ref=tot_x.at[source],
            send_sem=tx_send.at[source], recv_sem=tx_recv.at[source],
            device_id={"gx": source}, device_id_type=MESH)

    def total_y(i):
        to = lax.rem(my + i, m)
        return pltpu.make_async_remote_copy(
            src_ref=tot_y.at[my], dst_ref=tot_y.at[my],
            send_sem=ty_send.at[to], recv_sem=ty_recv.at[my],
            device_id={"gy": to}, device_id_type=MESH)

    def total_y_in(i):
        source = lax.rem(my + i, m)
        return pltpu.make_async_remote_copy(
            src_ref=tot_y.at[source], dst_ref=tot_y.at[source],
            send_sem=ty_send.at[source], recv_sem=ty_recv.at[source],
            device_id={"gy": source}, device_id_type=MESH)

    def each(count, action):
        def step(i, _):
            action(i)
            return 0

        lax.fori_loop(1, count, step, 0)

    each(n, lambda i: first(i).start())

    slots = cols.shape[1]
    owner = (
        lax.broadcasted_iota(jnp.int32, (LANES, slots), 0) == turb[...]
    ).astype(jnp.float32).astype(jnp.bfloat16)
    contract = (((1,), (1,)), ((), ()))
    counts = lax.dot_general(
        jnp.ones((BLOCK, slots), jnp.bfloat16), owner, contract, preferred_element_type=jnp.float32)

    def hit_plane(x, _):
        base = (me * width_x + x) * (width_y * m) + my * width_y
        column = lax.broadcasted_iota(jnp.int32, (width_y, slots), 0) + base
        match = (column == cols[...]).astype(jnp.float32).astype(jnp.bfloat16)
        hits[x] = lax.dot_general(match, owner, contract, preferred_element_type=jnp.float32)
        return 0

    lax.fori_loop(0, width_x, hit_plane, 0)

    pops_in.wait()

    def collide(x, b, acc):
        rows = pl.ds(pl.multiple_of(b * BLOCK, BLOCK), BLOCK)
        moments = forward([pops[i, x, rows, :] for i in range(27)])
        density = moments[0]
        inverse = 1.0 / density
        velocity = [moments[9] * inverse, moments[3] * inverse, moments[1] * inverse]
        row_sum = jnp.sum(velocity[0] * profile, axis=1, keepdims=True)
        acc = acc + row_sum * hits[x, rows, :]
        balance = balance_moments(density, velocity)
        relaxed = []
        for i in range(27):
            gap = moments[i] if balance[i] is None else moments[i] - balance[i]
            relaxed.append(moments[i] - rates[i] * gap)
        for i, value in enumerate(backward(relaxed)):
            post[i, x + 1, rows, :] = value
        return acc

    acc = lax.fori_loop(
        0, width_x,
        lambda x, acc: lax.fori_loop(0, blocks, lambda b, acc: collide(x, b, acc), acc),
        jnp.zeros((BLOCK, LANES), jnp.float32))

    tot_x[me] = jnp.broadcast_to(jnp.sum(acc, axis=0, keepdims=True), (BLOCK, LANES))
    each(n, lambda i: total_x(i).start())

    got[me] = mom[span(me), :]
    each(n, lambda i: first_in(i).wait_recv())

    def forward_chunk(i, _):
        to = lax.rem(me + i, n)
        stage[to] = got[pairing[to]]
        second(i).start()
        return 0

    lax.fori_loop(1, n, forward_chunk, 0)
    final[span(me), :] = got[pairing[me]]

    each(n, lambda i: total_x_in(i).wait_recv())
    tot_y[my] = lax.fori_loop(1, n, lambda i, t: t + tot_x[i], tot_x[0])
    each(m, lambda i: total_y(i).start())
    load_pad[...] = jnp.zeros((BLOCK, LANES), jnp.float32)
    load_pad[:, :turbines] = jnp.broadcast_to(loading[...], (BLOCK, turbines))
    norm = counts * jnp.sum(profile, axis=1, keepdims=True)
    each(m, lambda i: total_y_in(i).wait_recv())
    totals = lax.fori_loop(1, m, lambda i, t: t + tot_y[i], tot_y[0])
    disc_speed = totals / jnp.where(counts > 0.0, norm, 1.0)
    speed[...] = disc_speed[:1, :turbines]
    thrust = (0.5 * load_pad[...] * disc_speed * jnp.abs(disc_speed))[:1]

    def push(x, _):
        column = jnp.sum(hits[x] * thrust, axis=1, keepdims=True)
        kick = (-3.0 * column) * profile[:1]
        for i in range(9):
            post[i, x + 1] = post[i, x + 1] - kick
        for i in range(18, 27):
            post[i, x + 1] = post[i, x + 1] + kick
        return 0

    lax.fori_loop(0, width_x, push, 0)

    def x_copy(way):
        if way:
            src, dst, to = post.at[pl.ds(18, 9), width_x], post.at[pl.ds(18, 9), 0], right
        else:
            src, dst, to = post.at[pl.ds(0, 9), 1], post.at[pl.ds(0, 9), width_x + 1], left
        return pltpu.make_async_remote_copy(
            src_ref=src, dst_ref=dst, send_sem=x_send.at[way], recv_sem=x_recv.at[way],
            device_id={"gx": to}, device_id_type=MESH)

    def y_copy(way, late):
        planes = (0, fringe) if late else (fringe, width_x - fringe)
        return pltpu.make_async_remote_copy(
            src_ref=ysend.at[way, pl.ds(planes[0], planes[1])],
            dst_ref=yrecv.at[way, pl.ds(planes[0] + 1, planes[1])],
            send_sem=y_send.at[2 * way + late], recv_sem=y_recv.at[2 * way + late],
            device_id={"gy": above if way else below}, device_id_type=MESH)

    def corner_copy(way):
        if way:
            src, dst, to = yrecv.at[:, width_x, pl.ds(8, 8)], yrecv.at[:, 0, pl.ds(8, 8)], right
        else:
            src, dst, to = yrecv.at[:, 1, pl.ds(0, 8)], yrecv.at[:, width_x + 1, pl.ds(0, 8)], left
        return pltpu.make_async_remote_copy(
            src_ref=src, dst_ref=dst, send_sem=c_send.at[way], recv_sem=c_recv.at[way],
            device_id={"gx": to}, device_id_type=MESH)

    def pack(x, _):
        for way in range(2):
            edge = width_y - 1 if way else 0
            for kx in range(3):
                for kz in range(3):
                    row = row_of(kx, kz)
                    ysend[way, x, row : row + 1, :] = post[
                        9 * kx + 6 * way + kz, x + 1, edge : edge + 1, :]
        return 0

    lane = lax.broadcasted_iota(jnp.int32, (width_y, depth), 1)
    sub = lax.broadcasted_iota(jnp.int32, (width_y, depth), 0)

    def out_copy(x):
        return pltpu.make_async_copy(outv.at[:, x], out_hbm.at[:, x], out_sem.at[x])

    def stream(x, _):
        for i in range(27):
            kx, ky, kz = i // 9, (i // 3) % 3, i % 3
            source = x + 2 - kx
            moved = post[i, source]
            if ky != 1:
                way = 1 if ky == 2 else 0
                row = row_of(kx, kz)
                halo = yrecv[way, source, row : row + 1, :]
                moved = pltpu.roll(moved, 1 if way else width_y - 1, 0)
                moved = jnp.where(sub == (0 if way else width_y - 1), halo, moved)
            if kz != 1:
                moved = pltpu.roll(moved, 1 if kz == 2 else depth - 1, 1)
                moved = jnp.where(lane == (0 if kz == 2 else depth - 1), post[26 - i, x + 1], moved)
            outv[i, x] = moved
        out_copy(x).start()
        return 0

    x_copy(1).start()
    lax.fori_loop(fringe, width_x, pack, 0)
    for way in range(2):
        y_copy(way, 0).start()
    for way in range(2):
        y_copy(way, 0).wait_recv()
    corner_copy(1).start()
    lax.fori_loop(fringe + 1, width_x - 1, stream, 0)

    each(n, lambda i: second_in(i).wait_recv())
    for p in range(fringe):
        blend = 0.5 / (p + 1.0)

        def blend_block(b, _, p=p, blend=blend):
            rows = pl.ds(pl.multiple_of(b * BLOCK, BLOCK), BLOCK)
            low = []
            for q in range(10):
                start = pl.multiple_of((p * 10 + q) * width_y + b * BLOCK, BLOCK)
                low.append(final[pl.ds(start, BLOCK), :])
            for i, value in enumerate(rebuild(low)):
                post[i, p + 1, rows, :] = (1.0 - blend) * post[i, p + 1, rows, :] + blend * value
            return 0

        lax.fori_loop(0, blocks, blend_block, 0)
        if p == 0:
            x_copy(0).start()

    lax.fori_loop(0, fringe, pack, 0)
    for way in range(2):
        y_copy(way, 1).start()
    for way in range(2):
        y_copy(way, 1).wait_recv()
    corner_copy(0).start()
    x_copy(1).wait_recv()
    corner_copy(1).wait_recv()
    lax.fori_loop(0, fringe + 1, stream, 0)
    x_copy(0).wait_recv()
    corner_copy(0).wait_recv()
    lax.fori_loop(width_x - 1, width_x, stream, 0)

    each(n, lambda i: first(i).wait_send())
    each(n, lambda i: second(i).wait_send())
    each(n, lambda i: total_x(i).wait_send())
    each(m, lambda i: total_y(i).wait_send())
    for way in range(2):
        x_copy(way).wait_send()
        corner_copy(way).wait_send()
        for late in range(2):
            y_copy(way, late).wait_send()

    def drain(x, _):
        out_copy(x).wait()
        return 0

    lax.fori_loop(0, width_x, drain, 0)


def body(n, m, populations, precursor, pairing, rates, loading, disc_cols, disc_turb):
    comps, width_x, width_y, depth = populations.shape
    fringe = precursor.shape[1]
    rows = fringe * 10 * width_y
    chunk = -(-rows // (n * BLOCK)) * BLOCK
    turbines = loading.shape[0]
    slots = disc_cols.shape[0]
    f32 = jnp.float32
    anywhere = pl.BlockSpec(memory_space=pl.ANY)
    smem = pl.BlockSpec(memory_space=pltpu.SMEM)
    vmem = pl.BlockSpec(memory_space=pltpu.VMEM)
    dma = pltpu.SemaphoreType.DMA
    out, speed = pl.pallas_call(
        functools.partial(kernel, n, m, chunk),
        out_shape=(
            jax.ShapeDtypeStruct(populations.shape, f32),
            jax.ShapeDtypeStruct((1, turbines), f32),
        ),
        in_specs=[anywhere, anywhere, smem, smem, vmem, vmem, vmem],
        out_specs=(anywhere, vmem),
        scratch_shapes=[
            pltpu.VMEM(populations.shape, f32),
            pltpu.VMEM(precursor.shape, f32),
            pltpu.VMEM((comps, width_x + 2, width_y, depth), f32),
            pltpu.VMEM(populations.shape, f32),
            pltpu.VMEM((n * chunk, depth), f32),
            pltpu.VMEM((n, chunk, depth), f32),
            pltpu.VMEM((n, chunk, depth), f32),
            pltpu.VMEM((n * chunk, depth), f32),
            pltpu.VMEM((n, BLOCK, LANES), f32),
            pltpu.VMEM((m, BLOCK, LANES), f32),
            pltpu.VMEM((BLOCK, LANES), f32),
            pltpu.VMEM((width_x, width_y, LANES), f32),
            pltpu.VMEM((2, width_x, 16, depth), f32),
            pltpu.VMEM((2, width_x + 2, 16, depth), f32),
            dma((2,)), dma((width_x,)),
            dma((n,)), dma((n,)), dma((n,)), dma((n,)),
            dma((n,)), dma((n,)), dma((m,)), dma((m,)),
            dma((2,)), dma((2,)), dma((4,)), dma((4,)), dma((2,)), dma((2,)),
        ],
        compiler_params=pltpu.CompilerParams(
            collective_id=0, has_side_effects=True, vmem_limit_bytes=40 * 1024 * 1024),
    )(
        populations, precursor, pairing, rates,
        loading.reshape(1, turbines), disc_cols.reshape(1, slots), disc_turb.reshape(1, slots),
    )
    return out, speed.reshape(turbines)


def solution(mesh):
    n, m = mesh.shape["gx"], mesh.shape["gy"]
    in_specs = (P(None, "gx", "gy", None), P(None, "gx", "gy", None), P(), P(), P(), P(), P())
    out_specs = (P(None, "gx", "gy", None), P())
    return jax.shard_map(
        functools.partial(body, n, m), mesh=mesh, in_specs=in_specs, out_specs=out_specs, check_vma=False)
```

```python
import functools
import jax
import jax.numpy as jnp
import numpy as np
from jax import lax
from jax.experimental import pallas as pl
from jax.experimental.pallas import tpu as pltpu
from jax.sharding import PartitionSpec as P

MESH = pl.DeviceIdType.MESH
LANES = 128
BLOCK = 8
LOW = (0, 9, 3, 1, 18, 6, 2, 12, 10, 4)


def forward(cells):
    cells = list(cells)
    for stride in (9, 3, 1):
        for i in range(27):
            if (i // stride) % 3 == 0:
                low, mid, high = cells[i], cells[i + stride], cells[i + 2 * stride]
                even = (low + high) * (1.0 / 6.0)
                cells[i] = even + mid * (2.0 / 3.0)
                cells[i + stride] = (high - low) * (1.0 / 6.0)
                cells[i + 2 * stride] = even
    return cells


def backward(moments):
    cells = list(moments)
    for stride in (9, 3, 1):
        for i in range(27):
            if (i // stride) % 3 == 0:
                zero, one, two = cells[i], cells[i + stride], cells[i + 2 * stride]
                odd, even = one * 3.0, two * 3.0
                cells[i] = even - odd
                cells[i + stride] = (zero - two) * 1.5
                cells[i + 2 * stride] = even + odd
    return cells


def balance_moments(density, velocity):
    flux = [density * v for v in velocity]
    out = []
    for i in range(27):
        powers = (i // 9, (i // 3) % 3, i % 3)
        scale = (1.0 / 3.0) ** sum(p == 2 for p in powers)
        odd = [d for d in range(3) if powers[d] == 1]
        if len(odd) == 3:
            out.append(None)
            continue
        if len(odd) == 2:
            value = flux[odd[0]] * velocity[odd[1]]
        elif len(odd) == 1:
            value = flux[odd[0]]
        else:
            value = density
            for d in range(3):
                if powers[d] == 2:
                    value = value + 3.0 * (flux[d] * velocity[d])
        out.append(value if scale == 1.0 else value * scale)
    return out


def rebuild(low):
    rho, jx, jy, jz, xx, yy, zz, xy, xz, yz = low
    base = 2.5 * rho - 1.5 * (xx + yy + zz)
    third = rho * (1.0 / 3.0)
    linear = (3.0 * jx, 3.0 * jy, 3.0 * jz)
    square = (4.5 * (xx - third), 4.5 * (yy - third), 4.5 * (zz - third))
    cross = (9.0 * xy, 9.0 * xz, 9.0 * yz)

    def one(d, step):
        return square[d] + linear[d] if step > 0 else square[d] - linear[d]

    def signed(value, term, sign):
        return value + term if sign > 0 else value - term

    out = []
    for i in range(27):
        steps = (i // 9 - 1, (i // 3) % 3 - 1, i % 3 - 1)
        value = base
        for d in range(3):
            if steps[d]:
                value = value + one(d, steps[d])
        for (a, b), term in zip(((0, 1), (0, 2), (1, 2)), cross):
            if steps[a] * steps[b]:
                value = signed(value, term, steps[a] * steps[b])
        out.append(value)
    return out


def row_of(kx, kz):
    return kx * 3 + kz if kx < 2 else 8 + kz


def kernel(
    n, m, chunk,
    pops_hbm, prec_hbm, pairing_hbm, rates_hbm, loading_hbm, cols_hbm, turb_hbm,
    out_hbm, speed,
    pops, prec, pairing, rates, loading, cols, turb,
    post, outv, mom, stage, final, tot_x, tot_y, load_pad, hits, ysend, yrecv,
    in_sem, out_sem, a_send, a_recv, b_send, b_recv, tx_send, tx_recv, ty_send, ty_recv,
    x_send, x_recv, y_send, y_recv, c_send, c_recv, *got,
):
    comps, width_x, width_y, depth = pops.shape
    fringe = prec.shape[1]
    turbines = loading.shape[1]
    blocks = width_y // BLOCK
    me, my = lax.axis_index("gx"), lax.axis_index("gy")
    right, left = lax.rem(me + 1, n), lax.rem(me + n - 1, n)
    above, below = lax.rem(my + 1, m), lax.rem(my + m - 1, m)

    prec_in = [
        pltpu.make_async_copy(prec_hbm.at[:, p], prec.at[:, p], in_sem.at[p]) for p in range(fringe)]
    small_in = [
        pltpu.make_async_copy(source, target, in_sem.at[fringe + 1 + k])
        for k, (source, target) in enumerate((
            (cols_hbm, cols), (turb_hbm, turb), (pairing_hbm, pairing), (rates_hbm, rates),
            (loading_hbm, loading)))]
    pops_in = pltpu.make_async_copy(pops_hbm, pops, in_sem.at[fringe])
    for copy in prec_in + small_in + [pops_in]:
        copy.start()

    barrier = pltpu.get_barrier_semaphore()

    def greet_x(i, _):
        pl.semaphore_signal(barrier, inc=1, device_id={"gx": lax.rem(me + i, n)}, device_id_type=MESH)
        return 0

    def greet_y(i, _):
        pl.semaphore_signal(barrier, inc=1, device_id={"gy": lax.rem(my + i, m)}, device_id_type=MESH)
        return 0

    lax.fori_loop(1, n, greet_x, 0)
    lax.fori_loop(1, m, greet_y, 0)

    heights = lax.broadcasted_iota(jnp.int32, (BLOCK, depth), 1).astype(jnp.float32)
    profile = jnp.exp(-jnp.square((heights - depth / 3.0) / (depth / 6.0)))

    def span(j):
        return pl.ds(pl.multiple_of(j * chunk, BLOCK), chunk)

    def first(p, i, sent):
        other = lax.rem(me + i, n)
        slot = me if sent else other
        return pltpu.make_async_remote_copy(
            src_ref=mom.at[p, span(other), :], dst_ref=got[p].at[slot],
            send_sem=a_send.at[p * n + other], recv_sem=a_recv.at[p * n + slot],
            device_id={"gx": other}, device_id_type=MESH)

    def second(p, i, sent):
        other = lax.rem(me + i, n)
        slot = me if sent else other
        return pltpu.make_async_remote_copy(
            src_ref=stage.at[p, other], dst_ref=final.at[p, span(slot), :],
            send_sem=b_send.at[p * n + other], recv_sem=b_recv.at[p * n + slot],
            device_id={"gx": other}, device_id_type=MESH)

    def total_x(i, sent):
        other = lax.rem(me + i, n)
        slot = me if sent else other
        return pltpu.make_async_remote_copy(
            src_ref=tot_x.at[slot], dst_ref=tot_x.at[slot],
            send_sem=tx_send.at[other], recv_sem=tx_recv.at[slot],
            device_id={"gx": other}, device_id_type=MESH)

    def total_y(i, sent):
        other = lax.rem(my + i, m)
        slot = my if sent else other
        return pltpu.make_async_remote_copy(
            src_ref=tot_y.at[slot], dst_ref=tot_y.at[slot],
            send_sem=ty_send.at[other], recv_sem=ty_recv.at[slot],
            device_id={"gy": other}, device_id_type=MESH)

    def each(count, action):
        def step(i, _):
            action(i)
            return 0

        lax.fori_loop(1, count, step, 0)

    for p in range(fringe):
        prec_in[p].wait()

        def precursor_block(b, _, p=p):
            rows = pl.ds(pl.multiple_of(b * BLOCK, BLOCK), BLOCK)
            moments = forward([prec[i, p, rows, :] for i in range(27)])
            for q in range(10):
                start = pl.multiple_of(q * width_y + b * BLOCK, BLOCK)
                mom[p, pl.ds(start, BLOCK), :] = moments[LOW[q]]
            return 0

        lax.fori_loop(0, blocks, precursor_block, 0)
        if p == 0:
            pl.semaphore_wait(barrier, n + m - 2)
        each(n, lambda i, p=p: first(p, i, True).start())

    for copy in small_in:
        copy.wait()
    slots = cols.shape[1]
    owner = (
        lax.broadcasted_iota(jnp.int32, (LANES, slots), 0) == turb[...]
    ).astype(jnp.float32).astype(jnp.bfloat16)
    contract = (((1,), (1,)), ((), ()))
    counts = lax.dot_general(
        jnp.ones((BLOCK, slots), jnp.bfloat16), owner, contract, preferred_element_type=jnp.float32)
    shape = (width_x, width_y, slots)
    column = (
        (lax.broadcasted_iota(jnp.int32, shape, 0) + me * width_x) * (width_y * m)
        + lax.broadcasted_iota(jnp.int32, shape, 1) + my * width_y)
    match = (column == cols[...].reshape(1, 1, slots)).astype(jnp.float32).astype(jnp.bfloat16)
    hits[...] = lax.dot_general(
        match.reshape(width_x * width_y, slots), owner, contract, preferred_element_type=jnp.float32
    ).reshape(width_x, width_y, LANES)

    pops_in.wait()

    def share(x, acc):
        sheets = []
        for kx in range(3):
            c = [pops[9 * kx + k, x] for k in range(9)]
            corner = (c[0] + c[2]) + (c[6] + c[8])
            edge = (c[1] + c[3]) + (c[5] + c[7])
            sheets.append(corner * (1.0 / 36.0) + edge * (1.0 / 9.0) + c[4] * (4.0 / 9.0))
        density = (sheets[0] + sheets[2]) * (1.0 / 6.0) + sheets[1] * (2.0 / 3.0)
        velocity = (sheets[2] - sheets[0]) * (1.0 / 6.0) / density
        return acc + jnp.sum(velocity * profile[:1], axis=1, keepdims=True) * hits[x]

    acc = lax.fori_loop(0, width_x, share, jnp.zeros((width_y, LANES), jnp.float32))
    tot_x[me] = jnp.broadcast_to(jnp.sum(acc, axis=0, keepdims=True), (BLOCK, LANES))
    each(n, lambda i: total_x(i, True).start())

    def collide_block(x, b):
        rows = pl.ds(pl.multiple_of(b * BLOCK, BLOCK), BLOCK)
        moments = forward([pops[i, x, rows, :] for i in range(27)])
        density = moments[0]
        inverse = 1.0 / density
        velocity = [moments[9] * inverse, moments[3] * inverse, moments[1] * inverse]
        balance = balance_moments(density, velocity)
        relaxed = []
        for i in range(27):
            gap = moments[i] if balance[i] is None else moments[i] - balance[i]
            relaxed.append(moments[i] - rates[i] * gap)
        for i, value in enumerate(backward(relaxed)):
            post[i, x + 1, rows, :] = value

    def collide(start, stop):
        def step(k, _):
            collide_block(k // blocks, k % blocks)
            return 0

        lax.fori_loop(start * blocks, stop * blocks, step, 0)

    def pass_on(p):
        got[p][me] = mom[p, span(me), :]
        each(n, lambda i: first(p, i, False).wait_recv())

        def forward_chunk(i, _):
            to = lax.rem(me + i, n)
            stage[p, to] = got[p][pairing[to]]
            second(p, i, True).start()
            return 0

        lax.fori_loop(1, n, forward_chunk, 0)
        final[p, span(me), :] = got[p][pairing[me]]

    part = -(-width_x // (fringe + 1))
    for p in range(fringe):
        collide(p * part, (p + 1) * part)
        pass_on(p)

    each(n, lambda i: total_x(i, False).wait_recv())
    tot_y[my] = lax.fori_loop(1, n, lambda i, t: t + tot_x[i], tot_x[0])
    each(m, lambda i: total_y(i, True).start())
    collide(fringe * part, width_x)

    load_pad[...] = jnp.zeros((BLOCK, LANES), jnp.float32)
    load_pad[:, :turbines] = jnp.broadcast_to(loading[...], (BLOCK, turbines))
    norm = counts * jnp.sum(profile, axis=1, keepdims=True)
    each(m, lambda i: total_y(i, False).wait_recv())
    totals = lax.fori_loop(1, m, lambda i, t: t + tot_y[i], tot_y[0])
    disc_speed = totals / jnp.where(counts > 0.0, norm, 1.0)
    speed[...] = disc_speed[:1, :turbines]
    thrust = (0.5 * load_pad[...] * disc_speed * jnp.abs(disc_speed))[:1]

    def push(x, _):
        column = jnp.sum(hits[x] * thrust, axis=1, keepdims=True)
        kick = (-3.0 * column) * profile[:1]
        for i in range(9):
            post[i, x + 1] = post[i, x + 1] - kick
        for i in range(18, 27):
            post[i, x + 1] = post[i, x + 1] + kick
        return 0

    lax.fori_loop(0, width_x, push, 0)

    def x_copy(way):
        if way:
            src, dst, to = post.at[pl.ds(18, 9), width_x], post.at[pl.ds(18, 9), 0], right
        else:
            src, dst, to = post.at[pl.ds(0, 9), 1], post.at[pl.ds(0, 9), width_x + 1], left
        return pltpu.make_async_remote_copy(
            src_ref=src, dst_ref=dst, send_sem=x_send.at[way], recv_sem=x_recv.at[way],
            device_id={"gx": to}, device_id_type=MESH)

    def y_copy(way, late):
        planes = (0, fringe) if late else (fringe, width_x - fringe)
        return pltpu.make_async_remote_copy(
            src_ref=ysend.at[way, pl.ds(planes[0], planes[1])],
            dst_ref=yrecv.at[way, pl.ds(planes[0] + 1, planes[1])],
            send_sem=y_send.at[2 * way + late], recv_sem=y_recv.at[2 * way + late],
            device_id={"gy": above if way else below}, device_id_type=MESH)

    def corner_copy(way):
        if way:
            src, dst, to = yrecv.at[:, width_x, pl.ds(8, 8)], yrecv.at[:, 0, pl.ds(8, 8)], right
        else:
            src, dst, to = yrecv.at[:, 1, pl.ds(0, 8)], yrecv.at[:, width_x + 1, pl.ds(0, 8)], left
        return pltpu.make_async_remote_copy(
            src_ref=src, dst_ref=dst, send_sem=c_send.at[way], recv_sem=c_recv.at[way],
            device_id={"gx": to}, device_id_type=MESH)

    def pack(x, _):
        for way in range(2):
            edge = width_y - 1 if way else 0
            for kx in range(3):
                for kz in range(3):
                    row = row_of(kx, kz)
                    ysend[way, x, row : row + 1, :] = post[
                        9 * kx + 6 * way + kz, x + 1, edge : edge + 1, :]
        return 0

    lane = lax.broadcasted_iota(jnp.int32, (width_y, depth), 1)
    sub = lax.broadcasted_iota(jnp.int32, (width_y, depth), 0)

    def out_copy(x):
        return pltpu.make_async_copy(outv.at[:, x], out_hbm.at[:, x], out_sem.at[x])

    def stream(x, _):
        for i in range(27):
            kx, ky, kz = i // 9, (i // 3) % 3, i % 3
            source = x + 2 - kx
            moved = post[i, source]
            if ky != 1:
                way = 1 if ky == 2 else 0
                row = row_of(kx, kz)
                halo = yrecv[way, source, row : row + 1, :]
                moved = pltpu.roll(moved, 1 if way else width_y - 1, 0)
                moved = jnp.where(sub == (0 if way else width_y - 1), halo, moved)
            if kz != 1:
                moved = pltpu.roll(moved, 1 if kz == 2 else depth - 1, 1)
                moved = jnp.where(lane == (0 if kz == 2 else depth - 1), post[26 - i, x + 1], moved)
            outv[i, x] = moved
        out_copy(x).start()
        return 0

    x_copy(1).start()
    lax.fori_loop(fringe, width_x, pack, 0)
    for way in range(2):
        y_copy(way, 0).start()

    for p in range(fringe):
        blend = 0.5 / (p + 1.0)
        each(n, lambda i, p=p: second(p, i, False).wait_recv())

        def blend_block(b, _, p=p, blend=blend):
            rows = pl.ds(pl.multiple_of(b * BLOCK, BLOCK), BLOCK)
            low = []
            for q in range(10):
                start = pl.multiple_of(q * width_y + b * BLOCK, BLOCK)
                low.append(final[p, pl.ds(start, BLOCK), :])
            for i, value in enumerate(rebuild(low)):
                post[i, p + 1, rows, :] = (1.0 - blend) * post[i, p + 1, rows, :] + blend * value
            return 0

        lax.fori_loop(0, blocks, blend_block, 0)
        if p == 0:
            x_copy(0).start()

    lax.fori_loop(0, fringe, pack, 0)
    for way in range(2):
        y_copy(way, 1).start()
    for way in range(2):
        y_copy(way, 0).wait_recv()
    corner_copy(1).start()
    for way in range(2):
        y_copy(way, 1).wait_recv()
    corner_copy(0).start()
    lax.fori_loop(fringe + 1, width_x - 1, stream, 0)
    x_copy(1).wait_recv()
    corner_copy(1).wait_recv()
    lax.fori_loop(0, fringe + 1, stream, 0)
    x_copy(0).wait_recv()
    corner_copy(0).wait_recv()
    lax.fori_loop(width_x - 1, width_x, stream, 0)

    for p in range(fringe):
        each(n, lambda i, p=p: first(p, i, True).wait_send())
        each(n, lambda i, p=p: second(p, i, True).wait_send())
    each(n, lambda i: total_x(i, True).wait_send())
    each(m, lambda i: total_y(i, True).wait_send())
    for way in range(2):
        x_copy(way).wait_send()
        corner_copy(way).wait_send()
        for late in range(2):
            y_copy(way, late).wait_send()

    def drain(x, _):
        out_copy(x).wait()
        return 0

    lax.fori_loop(0, width_x, drain, 0)


def body(n, m, populations, precursor, pairing, rates, loading, disc_cols, disc_turb):
    comps, width_x, width_y, depth = populations.shape
    fringe = precursor.shape[1]
    rows = 10 * width_y
    chunk = -(-rows // (n * BLOCK)) * BLOCK
    turbines = loading.shape[0]
    slots = disc_cols.shape[0]
    f32 = jnp.float32
    anywhere = pl.BlockSpec(memory_space=pl.ANY)
    hbm = pl.BlockSpec(memory_space=pltpu.HBM)
    vmem = pl.BlockSpec(memory_space=pltpu.VMEM)
    dma = pltpu.SemaphoreType.DMA
    out, speed = pl.pallas_call(
        functools.partial(kernel, n, m, chunk),
        out_shape=(
            jax.ShapeDtypeStruct(populations.shape, f32),
            jax.ShapeDtypeStruct((1, turbines), f32),
        ),
        in_specs=[hbm] * 7,
        out_specs=(anywhere, vmem),
        scratch_shapes=[
            pltpu.VMEM(populations.shape, f32),
            pltpu.VMEM(precursor.shape, f32),
            pltpu.SMEM(pairing.shape, jnp.int32),
            pltpu.SMEM(rates.shape, f32),
            pltpu.VMEM((1, turbines), f32),
            pltpu.VMEM((1, slots), jnp.int32),
            pltpu.VMEM((1, slots), jnp.int32),
            pltpu.VMEM((comps, width_x + 2, width_y, depth), f32),
            pltpu.VMEM(populations.shape, f32),
            pltpu.VMEM((fringe, n * chunk, depth), f32),
            pltpu.VMEM((fringe, n, chunk, depth), f32),
            pltpu.VMEM((fringe, n * chunk, depth), f32),
            pltpu.VMEM((n, BLOCK, LANES), f32),
            pltpu.VMEM((m, BLOCK, LANES), f32),
            pltpu.VMEM((BLOCK, LANES), f32),
            pltpu.VMEM((width_x, width_y, LANES), f32),
            pltpu.VMEM((2, width_x, 16, depth), f32),
            pltpu.VMEM((2, width_x + 2, 16, depth), f32),
            dma((fringe + 6,)), dma((width_x,)),
            dma((fringe * n,)), dma((fringe * n,)), dma((fringe * n,)), dma((fringe * n,)),
            dma((n,)), dma((n,)), dma((m,)), dma((m,)),
            dma((2,)), dma((2,)), dma((4,)), dma((4,)), dma((2,)), dma((2,)),
        ] + [pltpu.VMEM((n, chunk, depth), f32)] * fringe,
        compiler_params=pltpu.CompilerParams(
            collective_id=0, has_side_effects=True, vmem_limit_bytes=64 * 1024 * 1024),
    )(
        populations, precursor, pairing, rates,
        loading.reshape(1, turbines), disc_cols.reshape(1, slots), disc_turb.reshape(1, slots),
    )
    return out, speed.reshape(turbines)


def solution(mesh):
    n, m = mesh.shape["gx"], mesh.shape["gy"]
    in_specs = (P(None, "gx", "gy", None), P(None, "gx", "gy", None), P(), P(), P(), P(), P())
    out_specs = (P(None, "gx", "gy", None), P())
    return jax.shard_map(
        functools.partial(body, n, m), mesh=mesh, in_specs=in_specs, out_specs=out_specs, check_vma=False)
```

```python
import functools
import jax
import jax.numpy as jnp
import numpy as np
from jax import lax
from jax.experimental import pallas as pl
from jax.experimental.pallas import tpu as pltpu
from jax.sharding import PartitionSpec as P

MESH = pl.DeviceIdType.MESH
LANES = 128
BLOCK = 8
LOW = (0, 9, 3, 1, 18, 6, 2, 12, 10, 4)


def forward(cells):
    cells = list(cells)
    for stride in (9, 3, 1):
        for i in range(27):
            if (i // stride) % 3 == 0:
                low, mid, high = cells[i], cells[i + stride], cells[i + 2 * stride]
                even = (low + high) * (1.0 / 6.0)
                cells[i] = even + mid * (2.0 / 3.0)
                cells[i + stride] = (high - low) * (1.0 / 6.0)
                cells[i + 2 * stride] = even
    return cells


def backward(moments):
    cells = list(moments)
    for stride in (9, 3, 1):
        for i in range(27):
            if (i // stride) % 3 == 0:
                zero, one, two = cells[i], cells[i + stride], cells[i + 2 * stride]
                odd, even = one * 3.0, two * 3.0
                cells[i] = even - odd
                cells[i + stride] = (zero - two) * 1.5
                cells[i + 2 * stride] = even + odd
    return cells


def balance_moments(density, velocity):
    flux = [density * v for v in velocity]
    out = []
    for i in range(27):
        powers = (i // 9, (i // 3) % 3, i % 3)
        scale = (1.0 / 3.0) ** sum(p == 2 for p in powers)
        odd = [d for d in range(3) if powers[d] == 1]
        if len(odd) == 3:
            out.append(None)
            continue
        if len(odd) == 2:
            value = flux[odd[0]] * velocity[odd[1]]
        elif len(odd) == 1:
            value = flux[odd[0]]
        else:
            value = density
            for d in range(3):
                if powers[d] == 2:
                    value = value + 3.0 * (flux[d] * velocity[d])
        out.append(value if scale == 1.0 else value * scale)
    return out


def rebuild(low):
    rho, jx, jy, jz, xx, yy, zz, xy, xz, yz = low
    base = 2.5 * rho - 1.5 * (xx + yy + zz)
    third = rho * (1.0 / 3.0)
    linear = (3.0 * jx, 3.0 * jy, 3.0 * jz)
    square = (4.5 * (xx - third), 4.5 * (yy - third), 4.5 * (zz - third))
    cross = (9.0 * xy, 9.0 * xz, 9.0 * yz)

    def one(d, step):
        return square[d] + linear[d] if step > 0 else square[d] - linear[d]

    def signed(value, term, sign):
        return value + term if sign > 0 else value - term

    out = []
    for i in range(27):
        steps = (i // 9 - 1, (i // 3) % 3 - 1, i % 3 - 1)
        value = base
        for d in range(3):
            if steps[d]:
                value = value + one(d, steps[d])
        for (a, b), term in zip(((0, 1), (0, 2), (1, 2)), cross):
            if steps[a] * steps[b]:
                value = signed(value, term, steps[a] * steps[b])
        out.append(value)
    return out


def row_of(kx, kz):
    return kx * 3 + kz if kx < 2 else 8 + kz


def kernel(
    n, m, chunk,
    pops_hbm, prec_hbm, pairing_hbm, rates_hbm, loading_hbm, cols_hbm, turb_hbm,
    out, speed,
    pops, prec, pairing, rates, loading, cols, turb,
    post, mom, stage, final, tot_x, tot_y, load_pad, hits, ysend, yrecv,
    in_sem, a_send, a_recv, b_send, b_recv, tx_send, tx_recv, ty_send, ty_recv,
    x_send, x_recv, y_send, y_recv, c_send, c_recv, *got,
):
    comps, width_x, width_y, depth = pops.shape
    fringe = prec.shape[1]
    turbines = loading.shape[1]
    blocks = width_y // BLOCK
    me, my = lax.axis_index("gx"), lax.axis_index("gy")
    right, left = lax.rem(me + 1, n), lax.rem(me + n - 1, n)
    above, below = lax.rem(my + 1, m), lax.rem(my + m - 1, m)

    prec_in = [
        pltpu.make_async_copy(prec_hbm.at[:, p], prec.at[:, p], in_sem.at[p]) for p in range(fringe)]
    small_in = [
        pltpu.make_async_copy(source, target, in_sem.at[fringe + 1 + k])
        for k, (source, target) in enumerate((
            (cols_hbm, cols), (turb_hbm, turb), (pairing_hbm, pairing), (rates_hbm, rates),
            (loading_hbm, loading)))]
    pops_in = pltpu.make_async_copy(pops_hbm, pops, in_sem.at[fringe])
    for copy in prec_in + small_in + [pops_in]:
        copy.start()

    barrier = pltpu.get_barrier_semaphore()

    def greet_x(i, _):
        pl.semaphore_signal(barrier, inc=1, device_id={"gx": lax.rem(me + i, n)}, device_id_type=MESH)
        return 0

    def greet_y(i, _):
        pl.semaphore_signal(barrier, inc=1, device_id={"gy": lax.rem(my + i, m)}, device_id_type=MESH)
        return 0

    lax.fori_loop(1, n, greet_x, 0)
    lax.fori_loop(1, m, greet_y, 0)

    heights = lax.broadcasted_iota(jnp.int32, (BLOCK, depth), 1).astype(jnp.float32)
    profile = jnp.exp(-jnp.square((heights - depth / 3.0) / (depth / 6.0)))

    def span(j):
        return pl.ds(pl.multiple_of(j * chunk, BLOCK), chunk)

    half = n // 2
    group, place = me // half, lax.rem(me, half)

    def partner(i):
        return lax.rem(group + 1 + i // half, 2) * half + lax.rem(place + i, half)

    def first(p, i, sent):
        other = partner(i)
        slot = me if sent else other
        return pltpu.make_async_remote_copy(
            src_ref=mom.at[p, span(lax.rem(other, half)), :], dst_ref=got[p].at[slot],
            send_sem=a_send.at[p * n + other], recv_sem=a_recv.at[p * n + slot],
            device_id={"gx": other}, device_id_type=MESH)

    def second(p, i, sent):
        other = lax.rem(place + i, half)
        slot = place if sent else other
        return pltpu.make_async_remote_copy(
            src_ref=stage.at[p, other], dst_ref=final.at[p, span(slot), :],
            send_sem=b_send.at[p * half + other], recv_sem=b_recv.at[p * half + slot],
            device_id={"gx": group * half + other}, device_id_type=MESH)

    def total_x(i, sent):
        other = lax.rem(me + i, n)
        slot = me if sent else other
        return pltpu.make_async_remote_copy(
            src_ref=tot_x.at[slot], dst_ref=tot_x.at[slot],
            send_sem=tx_send.at[other], recv_sem=tx_recv.at[slot],
            device_id={"gx": other}, device_id_type=MESH)

    def total_y(i, sent):
        other = lax.rem(my + i, m)
        slot = my if sent else other
        return pltpu.make_async_remote_copy(
            src_ref=tot_y.at[slot], dst_ref=tot_y.at[slot],
            send_sem=ty_send.at[other], recv_sem=ty_recv.at[slot],
            device_id={"gy": other}, device_id_type=MESH)

    def each(count, action):
        def step(i, _):
            action(i)
            return 0

        lax.fori_loop(1, count, step, 0)

    def partners(action):
        def step(i, _):
            action(i)
            return 0

        lax.fori_loop(0, half, step, 0)
        lax.fori_loop(half + 1, n, step, 0)

    for p in range(fringe):
        prec_in[p].wait()

        def precursor_block(b, _, p=p):
            rows = pl.ds(pl.multiple_of(b * BLOCK, BLOCK), BLOCK)
            moments = forward([prec[i, p, rows, :] for i in range(27)])
            for q in range(10):
                start = pl.multiple_of(q * width_y + b * BLOCK, BLOCK)
                mom[p, pl.ds(start, BLOCK), :] = moments[LOW[q]]
            return 0

        lax.fori_loop(0, blocks, precursor_block, 0)
        if p == 0:
            pl.semaphore_wait(barrier, n + m - 2)
        partners(lambda i, p=p: first(p, i, True).start())

    for copy in small_in:
        copy.wait()
    slots = cols.shape[1]
    owner = (
        lax.broadcasted_iota(jnp.int32, (LANES, slots), 0) == turb[...]
    ).astype(jnp.float32).astype(jnp.bfloat16)
    contract = (((1,), (1,)), ((), ()))
    counts = lax.dot_general(
        jnp.ones((BLOCK, slots), jnp.bfloat16), owner, contract, preferred_element_type=jnp.float32)
    shape = (width_x, width_y, slots)
    column = (
        (lax.broadcasted_iota(jnp.int32, shape, 0) + me * width_x) * (width_y * m)
        + lax.broadcasted_iota(jnp.int32, shape, 1) + my * width_y)
    match = (column == cols[...].reshape(1, 1, slots)).astype(jnp.float32).astype(jnp.bfloat16)
    hits[...] = lax.dot_general(
        match.reshape(width_x * width_y, slots), owner, contract, preferred_element_type=jnp.float32
    ).reshape(width_x, width_y, LANES)

    pops_in.wait()

    def share(x, acc):
        sheets = []
        for kx in range(3):
            c = [pops[9 * kx + k, x] for k in range(9)]
            corner = (c[0] + c[2]) + (c[6] + c[8])
            edge = (c[1] + c[3]) + (c[5] + c[7])
            sheets.append(corner * (1.0 / 36.0) + edge * (1.0 / 9.0) + c[4] * (4.0 / 9.0))
        density = (sheets[0] + sheets[2]) * (1.0 / 6.0) + sheets[1] * (2.0 / 3.0)
        velocity = (sheets[2] - sheets[0]) * (1.0 / 6.0) / density
        return acc + jnp.sum(velocity * profile[:1], axis=1, keepdims=True) * hits[x]

    acc = lax.fori_loop(0, width_x, share, jnp.zeros((width_y, LANES), jnp.float32))
    tot_x[me] = jnp.broadcast_to(jnp.sum(acc, axis=0, keepdims=True), (BLOCK, LANES))
    each(n, lambda i: total_x(i, True).start())

    def collide_block(x, b):
        rows = pl.ds(pl.multiple_of(b * BLOCK, BLOCK), BLOCK)
        moments = forward([pops[i, x, rows, :] for i in range(27)])
        density = moments[0]
        inverse = 1.0 / density
        velocity = [moments[9] * inverse, moments[3] * inverse, moments[1] * inverse]
        balance = balance_moments(density, velocity)
        relaxed = []
        for i in range(27):
            gap = moments[i] if balance[i] is None else moments[i] - balance[i]
            relaxed.append(moments[i] - rates[i] * gap)
        for i, value in enumerate(backward(relaxed)):
            post[i, x + 1, rows, :] = value

    def collide(start, stop):
        def step(k, _):
            collide_block(k // blocks, k % blocks)
            return 0

        lax.fori_loop(start * blocks, stop * blocks, step, 0)

    def pass_on(p):
        got[p][me] = mom[p, span(place), :]
        partners(lambda i: first(p, i, False).wait_recv())

        def forward_chunk(i, _):
            to = lax.rem(place + i, half)
            stage[p, to] = got[p][pairing[group * half + to]]
            second(p, i, True).start()
            return 0

        lax.fori_loop(1, half, forward_chunk, 0)
        final[p, span(place), :] = got[p][pairing[me]]

    part = -(-width_x // (fringe + 1))
    for p in range(fringe):
        collide(p * part, (p + 1) * part)
        pass_on(p)

    each(n, lambda i: total_x(i, False).wait_recv())
    tot_y[my] = lax.fori_loop(1, n, lambda i, t: t + tot_x[i], tot_x[0])
    each(m, lambda i: total_y(i, True).start())
    collide(fringe * part, width_x)

    load_pad[...] = jnp.zeros((BLOCK, LANES), jnp.float32)
    load_pad[:, :turbines] = jnp.broadcast_to(loading[...], (BLOCK, turbines))
    norm = counts * jnp.sum(profile, axis=1, keepdims=True)
    each(m, lambda i: total_y(i, False).wait_recv())
    totals = lax.fori_loop(1, m, lambda i, t: t + tot_y[i], tot_y[0])
    disc_speed = totals / jnp.where(counts > 0.0, norm, 1.0)
    speed[...] = disc_speed[:1, :turbines]
    thrust = (0.5 * load_pad[...] * disc_speed * jnp.abs(disc_speed))[:1]

    def push(x, _):
        column = jnp.sum(hits[x] * thrust, axis=1, keepdims=True)
        kick = (-3.0 * column) * profile[:1]
        for i in range(9):
            post[i, x + 1] = post[i, x + 1] - kick
        for i in range(18, 27):
            post[i, x + 1] = post[i, x + 1] + kick
        return 0

    lax.fori_loop(0, width_x, push, 0)

    def x_copy(way):
        if way:
            src, dst, to = post.at[pl.ds(18, 9), width_x], post.at[pl.ds(18, 9), 0], right
        else:
            src, dst, to = post.at[pl.ds(0, 9), 1], post.at[pl.ds(0, 9), width_x + 1], left
        return pltpu.make_async_remote_copy(
            src_ref=src, dst_ref=dst, send_sem=x_send.at[way], recv_sem=x_recv.at[way],
            device_id={"gx": to}, device_id_type=MESH)

    def y_copy(way, late):
        planes = (late - 1, 1) if late else (fringe, width_x - fringe)
        return pltpu.make_async_remote_copy(
            src_ref=ysend.at[way, pl.ds(planes[0], planes[1])],
            dst_ref=yrecv.at[way, pl.ds(planes[0] + 1, planes[1])],
            send_sem=y_send.at[(fringe + 1) * way + late], recv_sem=y_recv.at[(fringe + 1) * way + late],
            device_id={"gy": above if way else below}, device_id_type=MESH)

    def corner_copy(way):
        if way:
            src, dst, to = yrecv.at[:, width_x, pl.ds(8, 8)], yrecv.at[:, 0, pl.ds(8, 8)], right
        else:
            src, dst, to = yrecv.at[:, 1, pl.ds(0, 8)], yrecv.at[:, width_x + 1, pl.ds(0, 8)], left
        return pltpu.make_async_remote_copy(
            src_ref=src, dst_ref=dst, send_sem=c_send.at[way], recv_sem=c_recv.at[way],
            device_id={"gx": to}, device_id_type=MESH)

    def pack(x, _):
        for way in range(2):
            edge = width_y - 1 if way else 0
            for kx in range(3):
                for kz in range(3):
                    row = row_of(kx, kz)
                    ysend[way, x, row : row + 1, :] = post[
                        9 * kx + 6 * way + kz, x + 1, edge : edge + 1, :]
        return 0

    lane = lax.broadcasted_iota(jnp.int32, (width_y, depth), 1)
    sub = lax.broadcasted_iota(jnp.int32, (width_y, depth), 0)

    def stream(x, _):
        for i in range(27):
            kx, ky, kz = i // 9, (i // 3) % 3, i % 3
            source = x + 2 - kx
            moved = post[i, source]
            if ky != 1:
                way = 1 if ky == 2 else 0
                row = row_of(kx, kz)
                halo = yrecv[way, source, row : row + 1, :]
                moved = pltpu.roll(moved, 1 if way else width_y - 1, 0)
                moved = jnp.where(sub == (0 if way else width_y - 1), halo, moved)
            if kz != 1:
                moved = pltpu.roll(moved, 1 if kz == 2 else depth - 1, 1)
                moved = jnp.where(lane == (0 if kz == 2 else depth - 1), post[26 - i, x + 1], moved)
            out[i, x] = moved
        return 0

    x_copy(1).start()
    lax.fori_loop(fringe, width_x, pack, 0)
    for way in range(2):
        y_copy(way, 0).start()

    for p in range(fringe):
        blend = 0.5 / (p + 1.0)
        each(half, lambda i, p=p: second(p, i, False).wait_recv())

        def blend_block(b, _, p=p, blend=blend):
            rows = pl.ds(pl.multiple_of(b * BLOCK, BLOCK), BLOCK)
            low = []
            for q in range(10):
                start = pl.multiple_of(q * width_y + b * BLOCK, BLOCK)
                low.append(final[p, pl.ds(start, BLOCK), :])
            for i, value in enumerate(rebuild(low)):
                post[i, p + 1, rows, :] = (1.0 - blend) * post[i, p + 1, rows, :] + blend * value
            return 0

        lax.fori_loop(0, blocks, blend_block, 0)
        if p == 0:
            x_copy(0).start()
        pack(p, 0)
        for way in range(2):
            y_copy(way, p + 1).start()
        if p == 0:
            for way in range(2):
                y_copy(way, 0).wait_recv()
            corner_copy(1).start()

    for way in range(2):
        y_copy(way, 1).wait_recv()
    corner_copy(0).start()
    lax.fori_loop(fringe + 1, width_x - 1, stream, 0)
    for late in range(2, fringe + 1):
        for way in range(2):
            y_copy(way, late).wait_recv()
    x_copy(1).wait_recv()
    corner_copy(1).wait_recv()
    lax.fori_loop(0, fringe + 1, stream, 0)
    x_copy(0).wait_recv()
    corner_copy(0).wait_recv()
    lax.fori_loop(width_x - 1, width_x, stream, 0)

    for p in range(fringe):
        partners(lambda i, p=p: first(p, i, True).wait_send())
        each(half, lambda i, p=p: second(p, i, True).wait_send())
    each(n, lambda i: total_x(i, True).wait_send())
    each(m, lambda i: total_y(i, True).wait_send())
    for way in range(2):
        x_copy(way).wait_send()
        corner_copy(way).wait_send()
        for late in range(fringe + 1):
            y_copy(way, late).wait_send()


def body(n, m, populations, precursor, pairing, rates, loading, disc_cols, disc_turb):
    comps, width_x, width_y, depth = populations.shape
    fringe = precursor.shape[1]
    rows = 10 * width_y
    half = n // 2
    chunk = -(-rows // (half * BLOCK)) * BLOCK
    turbines = loading.shape[0]
    slots = disc_cols.shape[0]
    f32 = jnp.float32
    hbm = pl.BlockSpec(memory_space=pltpu.HBM)
    vmem = pl.BlockSpec(memory_space=pltpu.VMEM)
    dma = pltpu.SemaphoreType.DMA
    out, speed = pl.pallas_call(
        functools.partial(kernel, n, m, chunk),
        out_shape=(
            pltpu.VMEM(populations.shape, f32),
            jax.ShapeDtypeStruct((1, turbines), f32),
        ),
        in_specs=[hbm] * 7,
        out_specs=(vmem, vmem),
        scratch_shapes=[
            pltpu.VMEM(populations.shape, f32),
            pltpu.VMEM(precursor.shape, f32),
            pltpu.SMEM(pairing.shape, jnp.int32),
            pltpu.SMEM(rates.shape, f32),
            pltpu.VMEM((1, turbines), f32),
            pltpu.VMEM((1, slots), jnp.int32),
            pltpu.VMEM((1, slots), jnp.int32),
            pltpu.VMEM((comps, width_x + 2, width_y, depth), f32),
            pltpu.VMEM((fringe, half * chunk, depth), f32),
            pltpu.VMEM((fringe, half, chunk, depth), f32),
            pltpu.VMEM((fringe, half * chunk, depth), f32),
            pltpu.VMEM((n, BLOCK, LANES), f32),
            pltpu.VMEM((m, BLOCK, LANES), f32),
            pltpu.VMEM((BLOCK, LANES), f32),
            pltpu.VMEM((width_x, width_y, LANES), f32),
            pltpu.VMEM((2, width_x, 16, depth), f32),
            pltpu.VMEM((2, width_x + 2, 16, depth), f32),
            dma((fringe + 6,)),
            dma((fringe * n,)), dma((fringe * n,)), dma((fringe * half,)), dma((fringe * half,)),
            dma((n,)), dma((n,)), dma((m,)), dma((m,)),
            dma((2,)), dma((2,)), dma((2 * fringe + 2,)), dma((2 * fringe + 2,)), dma((2,)), dma((2,)),
        ] + [pltpu.VMEM((n, chunk, depth), f32)] * fringe,
        compiler_params=pltpu.CompilerParams(
            collective_id=0, has_side_effects=True, vmem_limit_bytes=40 * 1024 * 1024),
    )(*(pltpu.with_memory_space_constraint(x, pltpu.HBM) for x in (
        populations, precursor, pairing, rates,
        loading.reshape(1, turbines), disc_cols.reshape(1, slots), disc_turb.reshape(1, slots),
    )))
    return out, speed.reshape(turbines)


def solution(mesh):
    n, m = mesh.shape["gx"], mesh.shape["gy"]
    in_specs = (P(None, "gx", "gy", None), P(None, "gx", "gy", None), P(), P(), P(), P(), P())
    out_specs = (P(None, "gx", "gy", None), P())
    return jax.shard_map(
        functools.partial(body, n, m), mesh=mesh, in_specs=in_specs, out_specs=out_specs, check_vma=False)
```

```python
import functools
import jax
import jax.numpy as jnp
import numpy as np
from jax import lax
from jax.experimental import pallas as pl
from jax.experimental.pallas import tpu as pltpu
from jax.sharding import PartitionSpec as P

MESH = pl.DeviceIdType.MESH
LANES = 128
BLOCK = 8
LOW = (0, 9, 3, 1, 18, 6, 2, 12, 10, 4)


def forward(cells):
    cells = list(cells)
    for stride in (9, 3, 1):
        for i in range(27):
            if (i // stride) % 3 == 0:
                low, mid, high = cells[i], cells[i + stride], cells[i + 2 * stride]
                even = (low + high) * (1.0 / 6.0)
                cells[i] = even + mid * (2.0 / 3.0)
                cells[i + stride] = (high - low) * (1.0 / 6.0)
                cells[i + 2 * stride] = even
    return cells


def backward(moments):
    cells = list(moments)
    for stride in (9, 3, 1):
        for i in range(27):
            if (i // stride) % 3 == 0:
                zero, one, two = cells[i], cells[i + stride], cells[i + 2 * stride]
                odd, even = one * 3.0, two * 3.0
                cells[i] = even - odd
                cells[i + stride] = (zero - two) * 1.5
                cells[i + 2 * stride] = even + odd
    return cells


def balance_moments(density, velocity):
    flux = [density * v for v in velocity]
    out = []
    for i in range(27):
        powers = (i // 9, (i // 3) % 3, i % 3)
        scale = (1.0 / 3.0) ** sum(p == 2 for p in powers)
        odd = [d for d in range(3) if powers[d] == 1]
        if len(odd) == 3:
            out.append(None)
            continue
        if len(odd) == 2:
            value = flux[odd[0]] * velocity[odd[1]]
        elif len(odd) == 1:
            value = flux[odd[0]]
        else:
            value = density
            for d in range(3):
                if powers[d] == 2:
                    value = value + 3.0 * (flux[d] * velocity[d])
        out.append(value if scale == 1.0 else value * scale)
    return out


def rebuild(low, count=27):
    rho, jx, jy, jz, xx, yy, zz, xy, xz, yz = low
    base = 2.5 * rho - 1.5 * (xx + yy + zz)
    third = rho * (1.0 / 3.0)
    linear = (3.0 * jx, 3.0 * jy, 3.0 * jz)
    square = (4.5 * (xx - third), 4.5 * (yy - third), 4.5 * (zz - third))
    cross = (9.0 * xy, 9.0 * xz, 9.0 * yz)

    def one(d, step):
        return square[d] + linear[d] if step > 0 else square[d] - linear[d]

    def signed(value, term, sign):
        return value + term if sign > 0 else value - term

    out = []
    for i in range(count):
        steps = (i // 9 - 1, (i // 3) % 3 - 1, i % 3 - 1)
        value = base
        for d in range(3):
            if steps[d]:
                value = value + one(d, steps[d])
        for (a, b), term in zip(((0, 1), (0, 2), (1, 2)), cross):
            if steps[a] * steps[b]:
                value = signed(value, term, steps[a] * steps[b])
        out.append(value)
    return out


def row_of(kx, kz):
    return kx * 3 + kz if kx < 2 else 8 + kz


def kernel(
    n, m, chunk,
    pops_hbm, prec_hbm, pairing_hbm, rates_hbm, loading_hbm, cols_hbm, turb_hbm,
    out_any, speed,
    pops, prec, pairing, rates, loading, cols, turb,
    post, outv, mom, tot_x, tot_y, load_pad, hits, ysend, yrecv,
    in_sem, out_sem, a_send, a_recv, b_send, b_recv, tx_send, tx_recv, ty_send, ty_recv,
    x_send, x_recv, y_send, y_recv, *exchange,
):
    got, stage, final = exchange[0::3], exchange[1::3], exchange[2::3]
    comps, width_x, width_y, depth = pops.shape
    fringe = prec.shape[1]
    turbines = loading.shape[1]
    blocks = width_y // BLOCK
    me, my = lax.axis_index("gx"), lax.axis_index("gy")
    right, left = lax.rem(me + 1, n), lax.rem(me + n - 1, n)
    above, below = lax.rem(my + 1, m), lax.rem(my + m - 1, m)

    prec_in = [
        pltpu.make_async_copy(prec_hbm.at[:, p], prec.at[:, p], in_sem.at[p]) for p in range(fringe)]
    small_in = [
        pltpu.make_async_copy(source, target, in_sem.at[fringe + 1 + k])
        for k, (source, target) in enumerate((
            (cols_hbm, cols), (turb_hbm, turb), (pairing_hbm, pairing), (rates_hbm, rates),
            (loading_hbm, loading)))]
    pops_in = pltpu.make_async_copy(pops_hbm, pops, in_sem.at[fringe])
    for copy in prec_in + small_in + [pops_in]:
        copy.start()

    barrier = pltpu.get_barrier_semaphore()

    def greet_x(i, _):
        pl.semaphore_signal(barrier, inc=1, device_id={"gx": lax.rem(me + i, n)}, device_id_type=MESH)
        return 0

    def greet_y(i, _):
        pl.semaphore_signal(barrier, inc=1, device_id={"gy": lax.rem(my + i, m)}, device_id_type=MESH)
        return 0

    lax.fori_loop(1, n, greet_x, 0)
    lax.fori_loop(1, m, greet_y, 0)

    heights = lax.broadcasted_iota(jnp.int32, (BLOCK, depth), 1).astype(jnp.float32)
    profile = jnp.exp(-jnp.square((heights - depth / 3.0) / (depth / 6.0)))

    def span(j):
        return pl.ds(pl.multiple_of(j * chunk, BLOCK), chunk)

    half = n // 2
    group, place = me // half, lax.rem(me, half)

    def partner(i):
        return lax.rem(group + 1 + i // half, 2) * half + lax.rem(place + i, half)

    def first(p, i, sent):
        other = partner(i)
        slot = me if sent else other
        return pltpu.make_async_remote_copy(
            src_ref=mom.at[p, span(lax.rem(other, half)), :], dst_ref=got[p].at[slot],
            send_sem=a_send.at[p * n + other], recv_sem=a_recv.at[p * n + slot],
            device_id={"gx": other}, device_id_type=MESH)

    def second(p, i, sent):
        other = lax.rem(place + i, half)
        slot = place if sent else other
        return pltpu.make_async_remote_copy(
            src_ref=stage[p].at[other], dst_ref=final[p].at[:, span(slot), :],
            send_sem=b_send.at[p * half + other], recv_sem=b_recv.at[p * half + slot],
            device_id={"gx": group * half + other}, device_id_type=MESH)

    def total_x(i, sent):
        other = lax.rem(me + i, n)
        slot = me if sent else other
        return pltpu.make_async_remote_copy(
            src_ref=tot_x.at[slot], dst_ref=tot_x.at[slot],
            send_sem=tx_send.at[other], recv_sem=tx_recv.at[slot],
            device_id={"gx": other}, device_id_type=MESH)

    def total_y(i, sent):
        other = lax.rem(my + i, m)
        slot = my if sent else other
        return pltpu.make_async_remote_copy(
            src_ref=tot_y.at[slot], dst_ref=tot_y.at[slot],
            send_sem=ty_send.at[other], recv_sem=ty_recv.at[slot],
            device_id={"gy": other}, device_id_type=MESH)

    def each(count, action):
        def step(i, _):
            action(i)
            return 0

        lax.fori_loop(1, count, step, 0)

    def partners(action):
        def step(i, _):
            action(i)
            return 0

        lax.fori_loop(0, half, step, 0)
        lax.fori_loop(half + 1, n, step, 0)

    for p in range(fringe):
        prec_in[p].wait()

        def precursor_block(b, _, p=p):
            rows = pl.ds(pl.multiple_of(b * BLOCK, BLOCK), BLOCK)
            moments = forward([prec[i, p, rows, :] for i in range(27)])
            for q in range(10):
                start = pl.multiple_of(q * width_y + b * BLOCK, BLOCK)
                mom[p, pl.ds(start, BLOCK), :] = moments[LOW[q]]
            return 0

        lax.fori_loop(0, blocks, precursor_block, 0)
        if p == 0:
            pl.semaphore_wait(barrier, n + m - 2)
        partners(lambda i, p=p: first(p, i, True).start())

    for copy in small_in:
        copy.wait()
    slots = cols.shape[1]
    owner = (
        lax.broadcasted_iota(jnp.int32, (LANES, slots), 0) == turb[...]
    ).astype(jnp.float32).astype(jnp.bfloat16)
    contract = (((1,), (1,)), ((), ()))
    counts = lax.dot_general(
        jnp.ones((BLOCK, slots), jnp.bfloat16), owner, contract, preferred_element_type=jnp.float32)
    shape = (width_x, width_y, slots)
    column = (
        (lax.broadcasted_iota(jnp.int32, shape, 0) + me * width_x) * (width_y * m)
        + lax.broadcasted_iota(jnp.int32, shape, 1) + my * width_y)
    match = (column == cols[...].reshape(1, 1, slots)).astype(jnp.float32).astype(jnp.bfloat16)
    hits[...] = lax.dot_general(
        match.reshape(width_x * width_y, slots), owner, contract, preferred_element_type=jnp.float32
    ).reshape(width_x, width_y, LANES)

    pops_in.wait()

    def share(x, acc):
        sheets = []
        for kx in range(3):
            c = [pops[9 * kx + k, x] for k in range(9)]
            corner = (c[0] + c[2]) + (c[6] + c[8])
            edge = (c[1] + c[3]) + (c[5] + c[7])
            sheets.append(corner * (1.0 / 36.0) + edge * (1.0 / 9.0) + c[4] * (4.0 / 9.0))
        density = (sheets[0] + sheets[2]) * (1.0 / 6.0) + sheets[1] * (2.0 / 3.0)
        velocity = (sheets[2] - sheets[0]) * (1.0 / 6.0) / density
        return acc + jnp.sum(velocity * profile[:1], axis=1, keepdims=True) * hits[x]

    acc = lax.fori_loop(0, width_x, share, jnp.zeros((width_y, LANES), jnp.float32))
    tot_x[me] = jnp.broadcast_to(jnp.sum(acc, axis=0, keepdims=True), (BLOCK, LANES))
    each(n, lambda i: total_x(i, True).start())

    def collide_block(x, b):
        rows = pl.ds(pl.multiple_of(b * BLOCK, BLOCK), BLOCK)
        moments = forward([pops[i, x, rows, :] for i in range(27)])
        density = moments[0]
        inverse = 1.0 / density
        velocity = [moments[9] * inverse, moments[3] * inverse, moments[1] * inverse]
        balance = balance_moments(density, velocity)
        relaxed = []
        for i in range(27):
            gap = moments[i] if balance[i] is None else moments[i] - balance[i]
            relaxed.append(moments[i] - rates[i] * gap)
        for i, value in enumerate(backward(relaxed)):
            post[i, x + 1, rows, :] = value

    def collide(start, stop):
        def step(k, _):
            collide_block(k // blocks, k % blocks)
            return 0

        lax.fori_loop(start * blocks, stop * blocks, step, 0)

    def pass_on(p):
        got[p][me] = mom[p, span(place), :]
        partners(lambda i: first(p, i, False).wait_recv())

        def forward_chunk(i, _):
            to = lax.rem(place + i, half)
            stage[p][to, 0] = got[p][pairing[group * half + to]]
            if p == 0:
                stage[p][to, 1] = got[p][pairing[lax.rem(group * half + to + 1, n)]]
            second(p, i, True).start()
            return 0

        lax.fori_loop(1, half, forward_chunk, 0)
        final[p][0, span(place), :] = got[p][pairing[me]]
        if p == 0:
            final[p][1, span(place), :] = got[p][pairing[right]]

    part = -(-width_x // (fringe + 1))
    for p in range(fringe):
        collide(p * part, (p + 1) * part)
        pass_on(p)

    each(n, lambda i: total_x(i, False).wait_recv())
    tot_y[my] = lax.fori_loop(1, n, lambda i, t: t + tot_x[i], tot_x[0])
    each(m, lambda i: total_y(i, True).start())
    collide(fringe * part, width_x)

    load_pad[...] = jnp.zeros((BLOCK, LANES), jnp.float32)
    load_pad[:, :turbines] = jnp.broadcast_to(loading[...], (BLOCK, turbines))
    norm = counts * jnp.sum(profile, axis=1, keepdims=True)
    each(m, lambda i: total_y(i, False).wait_recv())
    totals = lax.fori_loop(1, m, lambda i, t: t + tot_y[i], tot_y[0])
    disc_speed = totals / jnp.where(counts > 0.0, norm, 1.0)
    speed[...] = disc_speed[:1, :turbines]
    thrust = (0.5 * load_pad[...] * disc_speed * jnp.abs(disc_speed))[:1]

    def push(x, _):
        column = jnp.sum(hits[x] * thrust, axis=1, keepdims=True)
        kick = (-3.0 * column) * profile[:1]
        for i in range(9):
            post[i, x + 1] = post[i, x + 1] - kick
        for i in range(18, 27):
            post[i, x + 1] = post[i, x + 1] + kick
        return 0

    lax.fori_loop(0, width_x, push, 0)

    def x_copy(way):
        if way:
            src, dst, to = post.at[pl.ds(18, 9), width_x], post.at[pl.ds(18, 9), 0], right
        else:
            src, dst, to = post.at[pl.ds(0, 9), 1], post.at[pl.ds(0, 9), width_x + 1], left
        return pltpu.make_async_remote_copy(
            src_ref=src, dst_ref=dst, send_sem=x_send.at[way], recv_sem=x_recv.at[way],
            device_id={"gx": to}, device_id_type=MESH)

    def y_slot(x):
        return lax.rem(x + 1, width_x + 2)

    def y_copy(way, late):
        slots = pl.ds(0, fringe + 2) if late else pl.ds(fringe + 2, width_x - fringe)
        return pltpu.make_async_remote_copy(
            src_ref=ysend.at[way, slots], dst_ref=yrecv.at[way, slots],
            send_sem=y_send.at[2 * way + late], recv_sem=y_recv.at[2 * way + late],
            device_id={"gy": above if way else below}, device_id_type=MESH)

    def pack(x, kinds=(0, 1, 2)):
        for way in range(2):
            edge = width_y - 1 if way else 0
            for kx in kinds:
                for kz in range(3):
                    row = row_of(kx, kz)
                    ysend[way, y_slot(x), row : row + 1, :] = post[
                        9 * kx + 6 * way + kz, x, edge : edge + 1, :]

    def pack_early(x, _):
        pack(x)
        return 0

    lane = lax.broadcasted_iota(jnp.int32, (width_y, depth), 1)
    sub = lax.broadcasted_iota(jnp.int32, (width_y, depth), 0)

    def out_copy(x):
        return pltpu.make_async_copy(outv.at[:, x], out_any.at[:, x], out_sem.at[x])

    def stream(x, _):
        for i in range(27):
            kx, ky, kz = i // 9, (i // 3) % 3, i % 3
            source = x + 2 - kx
            moved = post[i, source]
            if ky != 1:
                way = 1 if ky == 2 else 0
                row = row_of(kx, kz)
                halo = yrecv[way, y_slot(source), row : row + 1, :]
                moved = pltpu.roll(moved, 1 if way else width_y - 1, 0)
                moved = jnp.where(sub == (0 if way else width_y - 1), halo, moved)
            if kz != 1:
                moved = pltpu.roll(moved, 1 if kz == 2 else depth - 1, 1)
                moved = jnp.where(lane == (0 if kz == 2 else depth - 1), post[26 - i, x + 1], moved)
            outv[i, x] = moved
        out_copy(x).start()
        return 0

    for way in range(2):
        x_copy(way).start()
    lax.fori_loop(fringe + 1, width_x + 1, pack_early, 0)
    for way in range(2):
        y_copy(way, 0).start()
    for way in range(2):
        y_copy(way, 0).wait_recv()
    lax.fori_loop(fringe + 1, width_x - 1, stream, 0)

    def mix(p, table, x, count, b):
        blend = 0.5 / (p + 1.0)
        rows = pl.ds(pl.multiple_of(b * BLOCK, BLOCK), BLOCK)
        low = []
        for q in range(10):
            start = pl.multiple_of(q * width_y + b * BLOCK, BLOCK)
            low.append(final[p][table, pl.ds(start, BLOCK), :])
        for i, value in enumerate(rebuild(low, count)):
            post[i, x, rows, :] = (1.0 - blend) * post[i, x, rows, :] + blend * value

    def mixes(p, table, x, count):
        def step(b, _):
            mix(p, table, x, count, b)
            return 0

        lax.fori_loop(0, blocks, step, 0)

    x_copy(1).wait_recv()
    pack(0, (2,))
    each(half, lambda i: second(0, i, False).wait_recv())
    x_copy(0).wait_send()
    mixes(0, 0, 1, 27)
    x_copy(0).wait_recv()
    mixes(0, 1, width_x + 1, 9)
    pack(1)
    pack(width_x + 1, (0,))
    for p in range(1, fringe):
        each(half, lambda i, p=p: second(p, i, False).wait_recv())
        mixes(p, 0, p + 1, 27)
        pack(p + 1)
    for way in range(2):
        y_copy(way, 1).start()
    for way in range(2):
        y_copy(way, 1).wait_recv()
    lax.fori_loop(0, fringe + 1, stream, 0)
    lax.fori_loop(width_x - 1, width_x, stream, 0)

    for p in range(fringe):
        partners(lambda i, p=p: first(p, i, True).wait_send())
        each(half, lambda i, p=p: second(p, i, True).wait_send())
    each(n, lambda i: total_x(i, True).wait_send())
    each(m, lambda i: total_y(i, True).wait_send())
    x_copy(1).wait_send()
    for way in range(2):
        for late in range(2):
            y_copy(way, late).wait_send()

    def drain(x, _):
        out_copy(x).wait()
        return 0

    lax.fori_loop(0, width_x, drain, 0)


def body(n, m, populations, precursor, pairing, rates, loading, disc_cols, disc_turb):
    comps, width_x, width_y, depth = populations.shape
    fringe = precursor.shape[1]
    rows = 10 * width_y
    half = n // 2
    chunk = -(-rows // (half * BLOCK)) * BLOCK
    turbines = loading.shape[0]
    slots = disc_cols.shape[0]
    f32 = jnp.float32
    anywhere = pl.BlockSpec(memory_space=pl.ANY)
    hbm = pl.BlockSpec(memory_space=pltpu.HBM)
    vmem = pl.BlockSpec(memory_space=pltpu.VMEM)
    dma = pltpu.SemaphoreType.DMA
    out, speed = pl.pallas_call(
        functools.partial(kernel, n, m, chunk),
        out_shape=(
            pltpu.VMEM(populations.shape, f32),
            jax.ShapeDtypeStruct((1, turbines), f32),
        ),
        in_specs=[hbm] * 7,
        out_specs=(anywhere, vmem),
        scratch_shapes=[
            pltpu.VMEM(populations.shape, f32),
            pltpu.VMEM(precursor.shape, f32),
            pltpu.SMEM(pairing.shape, jnp.int32),
            pltpu.SMEM(rates.shape, f32),
            pltpu.VMEM((1, turbines), f32),
            pltpu.VMEM((1, slots), jnp.int32),
            pltpu.VMEM((1, slots), jnp.int32),
            pltpu.VMEM((comps, width_x + 2, width_y, depth), f32),
            pltpu.VMEM(populations.shape, f32),
            pltpu.VMEM((fringe, half * chunk, depth), f32),
            pltpu.VMEM((n, BLOCK, LANES), f32),
            pltpu.VMEM((m, BLOCK, LANES), f32),
            pltpu.VMEM((BLOCK, LANES), f32),
            pltpu.VMEM((width_x, width_y, LANES), f32),
            pltpu.VMEM((2, width_x + 2, 16, depth), f32),
            pltpu.VMEM((2, width_x + 2, 16, depth), f32),
            dma((fringe + 6,)), dma((width_x,)),
            dma((fringe * n,)), dma((fringe * n,)), dma((fringe * half,)), dma((fringe * half,)),
            dma((n,)), dma((n,)), dma((m,)), dma((m,)),
            dma((2,)), dma((2,)), dma((4,)), dma((4,)),
        ] + [
            pltpu.VMEM(shape, f32)
            for p in range(fringe)
            for shape in (
                (n, chunk, depth),
                (half, 1 + (p == 0), chunk, depth),
                (1 + (p == 0), half * chunk, depth))
        ],
        compiler_params=pltpu.CompilerParams(
            collective_id=0, has_side_effects=True, vmem_limit_bytes=40 * 1024 * 1024),
    )(*(pltpu.with_memory_space_constraint(x, pltpu.HBM) for x in (
        populations, precursor, pairing, rates,
        loading.reshape(1, turbines), disc_cols.reshape(1, slots), disc_turb.reshape(1, slots),
    )))
    return out, speed.reshape(turbines)


def solution(mesh):
    n, m = mesh.shape["gx"], mesh.shape["gy"]
    in_specs = (P(None, "gx", "gy", None), P(None, "gx", "gy", None), P(), P(), P(), P(), P())
    out_specs = (P(None, "gx", "gy", None), P())
    return jax.shard_map(
        functools.partial(body, n, m), mesh=mesh, in_specs=in_specs, out_specs=out_specs, check_vma=False)
```

```python
import functools
import jax
import jax.numpy as jnp
import numpy as np
from jax import lax
from jax.experimental import pallas as pl
from jax.experimental.pallas import tpu as pltpu
from jax.sharding import PartitionSpec as P

MESH = pl.DeviceIdType.MESH
LANES = 128
BLOCK = 8
LOW = (0, 9, 3, 1, 18, 6, 2, 12, 10, 4)


def forward(cells):
    cells = list(cells)
    for stride in (9, 3, 1):
        for i in range(27):
            if (i // stride) % 3 == 0:
                low, mid, high = cells[i], cells[i + stride], cells[i + 2 * stride]
                even = (low + high) * (1.0 / 6.0)
                cells[i] = even + mid * (2.0 / 3.0)
                cells[i + stride] = (high - low) * (1.0 / 6.0)
                cells[i + 2 * stride] = even
    return cells


def backward(moments):
    cells = list(moments)
    for stride in (9, 3, 1):
        for i in range(27):
            if (i // stride) % 3 == 0:
                zero, one, two = cells[i], cells[i + stride], cells[i + 2 * stride]
                odd, even = one * 3.0, two * 3.0
                cells[i] = even - odd
                cells[i + stride] = (zero - two) * 1.5
                cells[i + 2 * stride] = even + odd
    return cells


def balance_moments(density, velocity):
    flux = [density * v for v in velocity]
    out = []
    for i in range(27):
        powers = (i // 9, (i // 3) % 3, i % 3)
        scale = (1.0 / 3.0) ** sum(p == 2 for p in powers)
        odd = [d for d in range(3) if powers[d] == 1]
        if len(odd) == 3:
            out.append(None)
            continue
        if len(odd) == 2:
            value = flux[odd[0]] * velocity[odd[1]]
        elif len(odd) == 1:
            value = flux[odd[0]]
        else:
            value = density
            for d in range(3):
                if powers[d] == 2:
                    value = value + 3.0 * (flux[d] * velocity[d])
        out.append(value if scale == 1.0 else value * scale)
    return out


def rebuild(low):
    rho, jx, jy, jz, xx, yy, zz, xy, xz, yz = low
    base = 2.5 * rho - 1.5 * (xx + yy + zz)
    third = rho * (1.0 / 3.0)
    linear = (3.0 * jx, 3.0 * jy, 3.0 * jz)
    square = (4.5 * (xx - third), 4.5 * (yy - third), 4.5 * (zz - third))
    cross = (9.0 * xy, 9.0 * xz, 9.0 * yz)

    def one(d, step):
        return square[d] + linear[d] if step > 0 else square[d] - linear[d]

    def signed(value, term, sign):
        return value + term if sign > 0 else value - term

    out = []
    for i in range(27):
        steps = (i // 9 - 1, (i // 3) % 3 - 1, i % 3 - 1)
        value = base
        for d in range(3):
            if steps[d]:
                value = value + one(d, steps[d])
        for (a, b), term in zip(((0, 1), (0, 2), (1, 2)), cross):
            if steps[a] * steps[b]:
                value = signed(value, term, steps[a] * steps[b])
        out.append(value)
    return out


def row_of(kx, kz):
    return kx * 3 + kz if kx < 2 else 8 + kz


def kernel(
    n, m, chunk,
    pops_hbm, prec_hbm, pairing_hbm, rates_hbm, loading_hbm, cols_hbm, turb_hbm,
    out_hbm, speed,
    pops, prec, pairing, rates, loading, cols, turb,
    post, outv, mom, stage, final, tot_x, tot_y, load_pad, hits, ysend, yrecv,
    in_sem, out_sem, a_send, a_recv, b_send, b_recv, tx_send, tx_recv, ty_send, ty_recv,
    x_send, x_recv, y_send, y_recv, c_send, c_recv, *got,
):
    comps, width_x, width_y, depth = pops.shape
    fringe = prec.shape[1]
    turbines = loading.shape[1]
    blocks = width_y // BLOCK
    me, my = lax.axis_index("gx"), lax.axis_index("gy")
    right, left = lax.rem(me + 1, n), lax.rem(me + n - 1, n)
    above, below = lax.rem(my + 1, m), lax.rem(my + m - 1, m)

    prec_in = [
        pltpu.make_async_copy(prec_hbm.at[:, p], prec.at[:, p], in_sem.at[p]) for p in range(fringe)]
    small_in = [
        pltpu.make_async_copy(source, target, in_sem.at[fringe + 1 + k])
        for k, (source, target) in enumerate((
            (cols_hbm, cols), (turb_hbm, turb), (pairing_hbm, pairing), (rates_hbm, rates),
            (loading_hbm, loading)))]
    pops_in = pltpu.make_async_copy(pops_hbm, pops, in_sem.at[fringe])
    for copy in prec_in + small_in + [pops_in]:
        copy.start()

    barrier = pltpu.get_barrier_semaphore()

    def greet_x(i, _):
        pl.semaphore_signal(barrier, inc=1, device_id={"gx": lax.rem(me + i, n)}, device_id_type=MESH)
        return 0

    def greet_y(i, _):
        pl.semaphore_signal(barrier, inc=1, device_id={"gy": lax.rem(my + i, m)}, device_id_type=MESH)
        return 0

    lax.fori_loop(1, n, greet_x, 0)
    lax.fori_loop(1, m, greet_y, 0)

    heights = lax.broadcasted_iota(jnp.int32, (BLOCK, depth), 1).astype(jnp.float32)
    profile = jnp.exp(-jnp.square((heights - depth / 3.0) / (depth / 6.0)))

    def span(j):
        return pl.ds(pl.multiple_of(j * chunk, BLOCK), chunk)

    def first(p, i, sent):
        other = lax.rem(me + i, n)
        slot = me if sent else other
        return pltpu.make_async_remote_copy(
            src_ref=mom.at[p, span(other), :], dst_ref=got[p].at[slot],
            send_sem=a_send.at[p * n + other], recv_sem=a_recv.at[p * n + slot],
            device_id={"gx": other}, device_id_type=MESH)

    def second(p, i, sent):
        other = lax.rem(me + i, n)
        slot = me if sent else other
        return pltpu.make_async_remote_copy(
            src_ref=stage.at[p, other], dst_ref=final.at[p, span(slot), :],
            send_sem=b_send.at[p * n + other], recv_sem=b_recv.at[p * n + slot],
            device_id={"gx": other}, device_id_type=MESH)

    def total_x(i, sent):
        other = lax.rem(me + i, n)
        slot = me if sent else other
        return pltpu.make_async_remote_copy(
            src_ref=tot_x.at[slot], dst_ref=tot_x.at[slot],
            send_sem=tx_send.at[other], recv_sem=tx_recv.at[slot],
            device_id={"gx": other}, device_id_type=MESH)

    def total_y(i, sent):
        other = lax.rem(my + i, m)
        slot = my if sent else other
        return pltpu.make_async_remote_copy(
            src_ref=tot_y.at[slot], dst_ref=tot_y.at[slot],
            send_sem=ty_send.at[other], recv_sem=ty_recv.at[slot],
            device_id={"gy": other}, device_id_type=MESH)

    def each(count, action):
        def step(i, _):
            action(i)
            return 0

        lax.fori_loop(1, count, step, 0)

    for p in range(fringe):
        prec_in[p].wait()

        def precursor_block(b, _, p=p):
            rows = pl.ds(pl.multiple_of(b * BLOCK, BLOCK), BLOCK)
            moments = forward([prec[i, p, rows, :] for i in range(27)])
            for q in range(10):
                start = pl.multiple_of(q * width_y + b * BLOCK, BLOCK)
                mom[p, pl.ds(start, BLOCK), :] = moments[LOW[q]]
            return 0

        lax.fori_loop(0, blocks, precursor_block, 0)
        if p == 0:
            pl.semaphore_wait(barrier, n + m - 2)
        each(n, lambda i, p=p: first(p, i, True).start())

    for copy in small_in:
        copy.wait()
    slots = cols.shape[1]
    owner = (
        lax.broadcasted_iota(jnp.int32, (LANES, slots), 0) == turb[...]
    ).astype(jnp.float32).astype(jnp.bfloat16)
    contract = (((1,), (1,)), ((), ()))
    counts = lax.dot_general(
        jnp.ones((BLOCK, slots), jnp.bfloat16), owner, contract, preferred_element_type=jnp.float32)
    shape = (width_x, width_y, slots)
    column = (
        (lax.broadcasted_iota(jnp.int32, shape, 0) + me * width_x) * (width_y * m)
        + lax.broadcasted_iota(jnp.int32, shape, 1) + my * width_y)
    match = (column == cols[...].reshape(1, 1, slots)).astype(jnp.float32).astype(jnp.bfloat16)
    hits[...] = lax.dot_general(
        match.reshape(width_x * width_y, slots), owner, contract, preferred_element_type=jnp.float32
    ).reshape(width_x, width_y, LANES)

    pops_in.wait()

    def share(x, acc):
        sheets = []
        for kx in range(3):
            c = [pops[9 * kx + k, x] for k in range(9)]
            corner = (c[0] + c[2]) + (c[6] + c[8])
            edge = (c[1] + c[3]) + (c[5] + c[7])
            sheets.append(corner * (1.0 / 36.0) + edge * (1.0 / 9.0) + c[4] * (4.0 / 9.0))
        density = (sheets[0] + sheets[2]) * (1.0 / 6.0) + sheets[1] * (2.0 / 3.0)
        velocity = (sheets[2] - sheets[0]) * (1.0 / 6.0) / density
        return acc + jnp.sum(velocity * profile[:1], axis=1, keepdims=True) * hits[x]

    acc = lax.fori_loop(0, width_x, share, jnp.zeros((width_y, LANES), jnp.float32))
    tot_x[me] = jnp.broadcast_to(jnp.sum(acc, axis=0, keepdims=True), (BLOCK, LANES))
    each(n, lambda i: total_x(i, True).start())

    def collide_block(x, b):
        rows = pl.ds(pl.multiple_of(b * BLOCK, BLOCK), BLOCK)
        moments = forward([pops[i, x, rows, :] for i in range(27)])
        density = moments[0]
        inverse = 1.0 / density
        velocity = [moments[9] * inverse, moments[3] * inverse, moments[1] * inverse]
        balance = balance_moments(density, velocity)
        relaxed = []
        for i in range(27):
            gap = moments[i] if balance[i] is None else moments[i] - balance[i]
            relaxed.append(moments[i] - rates[i] * gap)
        for i, value in enumerate(backward(relaxed)):
            post[i, x + 1, rows, :] = value

    def collide(start, stop):
        def step(k, _):
            collide_block(k // blocks, k % blocks)
            return 0

        lax.fori_loop(start * blocks, stop * blocks, step, 0)

    def pass_on(p):
        got[p][me] = mom[p, span(me), :]
        each(n, lambda i: first(p, i, False).wait_recv())

        def forward_chunk(i, _):
            to = lax.rem(me + i, n)
            stage[p, to] = got[p][pairing[to]]
            second(p, i, True).start()
            return 0

        lax.fori_loop(1, n, forward_chunk, 0)
        final[p, span(me), :] = got[p][pairing[me]]

    part = -(-width_x // (fringe + 1))
    for p in range(fringe):
        collide(p * part, (p + 1) * part)
        pass_on(p)

    each(n, lambda i: total_x(i, False).wait_recv())
    tot_y[my] = lax.fori_loop(1, n, lambda i, t: t + tot_x[i], tot_x[0])
    each(m, lambda i: total_y(i, True).start())
    collide(fringe * part, width_x)

    load_pad[...] = jnp.zeros((BLOCK, LANES), jnp.float32)
    load_pad[:, :turbines] = jnp.broadcast_to(loading[...], (BLOCK, turbines))
    norm = counts * jnp.sum(profile, axis=1, keepdims=True)
    each(m, lambda i: total_y(i, False).wait_recv())
    totals = lax.fori_loop(1, m, lambda i, t: t + tot_y[i], tot_y[0])
    disc_speed = totals / jnp.where(counts > 0.0, norm, 1.0)
    speed[...] = disc_speed[:1, :turbines]
    thrust = (0.5 * load_pad[...] * disc_speed * jnp.abs(disc_speed))[:1]

    def push(x, _):
        column = jnp.sum(hits[x] * thrust, axis=1, keepdims=True)
        kick = (-3.0 * column) * profile[:1]
        for i in range(9):
            post[i, x + 1] = post[i, x + 1] - kick
        for i in range(18, 27):
            post[i, x + 1] = post[i, x + 1] + kick
        return 0

    lax.fori_loop(0, width_x, push, 0)

    def x_copy(way):
        if way:
            src, dst, to = post.at[pl.ds(18, 9), width_x], post.at[pl.ds(18, 9), 0], right
        else:
            src, dst, to = post.at[pl.ds(0, 9), 1], post.at[pl.ds(0, 9), width_x + 1], left
        return pltpu.make_async_remote_copy(
            src_ref=src, dst_ref=dst, send_sem=x_send.at[way], recv_sem=x_recv.at[way],
            device_id={"gx": to}, device_id_type=MESH)

    def y_copy(way, late):
        planes = (0, fringe) if late else (fringe, width_x - fringe)
        return pltpu.make_async_remote_copy(
            src_ref=ysend.at[way, pl.ds(planes[0], planes[1])],
            dst_ref=yrecv.at[way, pl.ds(planes[0] + 1, planes[1])],
            send_sem=y_send.at[2 * way + late], recv_sem=y_recv.at[2 * way + late],
            device_id={"gy": above if way else below}, device_id_type=MESH)

    def corner_copy(way):
        if way:
            src, dst, to = yrecv.at[:, width_x, pl.ds(8, 8)], yrecv.at[:, 0, pl.ds(8, 8)], right
        else:
            src, dst, to = yrecv.at[:, 1, pl.ds(0, 8)], yrecv.at[:, width_x + 1, pl.ds(0, 8)], left
        return pltpu.make_async_remote_copy(
            src_ref=src, dst_ref=dst, send_sem=c_send.at[way], recv_sem=c_recv.at[way],
            device_id={"gx": to}, device_id_type=MESH)

    def pack(x, _):
        for way in range(2):
            edge = width_y - 1 if way else 0
            for kx in range(3):
                for kz in range(3):
                    row = row_of(kx, kz)
                    ysend[way, x, row : row + 1, :] = post[
                        9 * kx + 6 * way + kz, x + 1, edge : edge + 1, :]
        return 0

    lane = lax.broadcasted_iota(jnp.int32, (width_y, depth), 1)
    sub = lax.broadcasted_iota(jnp.int32, (width_y, depth), 0)

    def out_copy(x):
        return pltpu.make_async_copy(outv.at[:, x], out_hbm.at[:, x], out_sem.at[x])

    def stream(x, _):
        for i in range(27):
            kx, ky, kz = i // 9, (i // 3) % 3, i % 3
            source = x + 2 - kx
            moved = post[i, source]
            if ky != 1:
                way = 1 if ky == 2 else 0
                row = row_of(kx, kz)
                halo = yrecv[way, source, row : row + 1, :]
                moved = pltpu.roll(moved, 1 if way else width_y - 1, 0)
                moved = jnp.where(sub == (0 if way else width_y - 1), halo, moved)
            if kz != 1:
                moved = pltpu.roll(moved, 1 if kz == 2 else depth - 1, 1)
                moved = jnp.where(lane == (0 if kz == 2 else depth - 1), post[26 - i, x + 1], moved)
            outv[i, x] = moved
        out_copy(x).start()
        return 0

    x_copy(1).start()
    lax.fori_loop(fringe, width_x, pack, 0)
    for way in range(2):
        y_copy(way, 0).start()

    for p in range(fringe):
        blend = 0.5 / (p + 1.0)
        each(n, lambda i, p=p: second(p, i, False).wait_recv())

        def blend_block(b, _, p=p, blend=blend):
            rows = pl.ds(pl.multiple_of(b * BLOCK, BLOCK), BLOCK)
            low = []
            for q in range(10):
                start = pl.multiple_of(q * width_y + b * BLOCK, BLOCK)
                low.append(final[p, pl.ds(start, BLOCK), :])
            for i, value in enumerate(rebuild(low)):
                post[i, p + 1, rows, :] = (1.0 - blend) * post[i, p + 1, rows, :] + blend * value
            return 0

        lax.fori_loop(0, blocks, blend_block, 0)
        if p == 0:
            x_copy(0).start()

    lax.fori_loop(0, fringe, pack, 0)
    for way in range(2):
        y_copy(way, 1).start()
    for way in range(2):
        y_copy(way, 0).wait_recv()
    corner_copy(1).start()
    for way in range(2):
        y_copy(way, 1).wait_recv()
    corner_copy(0).start()
    lax.fori_loop(fringe + 1, width_x - 1, stream, 0)
    x_copy(1).wait_recv()
    corner_copy(1).wait_recv()
    lax.fori_loop(0, fringe + 1, stream, 0)
    x_copy(0).wait_recv()
    corner_copy(0).wait_recv()
    lax.fori_loop(width_x - 1, width_x, stream, 0)

    for p in range(fringe):
        each(n, lambda i, p=p: first(p, i, True).wait_send())
        each(n, lambda i, p=p: second(p, i, True).wait_send())
    each(n, lambda i: total_x(i, True).wait_send())
    each(m, lambda i: total_y(i, True).wait_send())
    for way in range(2):
        x_copy(way).wait_send()
        corner_copy(way).wait_send()
        for late in range(2):
            y_copy(way, late).wait_send()

    def drain(x, _):
        out_copy(x).wait()
        return 0

    lax.fori_loop(0, width_x, drain, 0)


def body(n, m, populations, precursor, pairing, rates, loading, disc_cols, disc_turb):
    comps, width_x, width_y, depth = populations.shape
    fringe = precursor.shape[1]
    rows = 10 * width_y
    chunk = -(-rows // (n * BLOCK)) * BLOCK
    turbines = loading.shape[0]
    slots = disc_cols.shape[0]
    f32 = jnp.float32
    anywhere = pl.BlockSpec(memory_space=pl.ANY)
    hbm = pl.BlockSpec(memory_space=pltpu.HBM)
    vmem = pl.BlockSpec(memory_space=pltpu.VMEM)
    dma = pltpu.SemaphoreType.DMA
    out, speed = pl.pallas_call(
        functools.partial(kernel, n, m, chunk),
        out_shape=(
            pltpu.VMEM(populations.shape, f32),
            jax.ShapeDtypeStruct((1, turbines), f32),
        ),
        in_specs=[hbm] * 7,
        out_specs=(anywhere, vmem),
        scratch_shapes=[
            pltpu.VMEM(populations.shape, f32),
            pltpu.VMEM(precursor.shape, f32),
            pltpu.SMEM(pairing.shape, jnp.int32),
            pltpu.SMEM(rates.shape, f32),
            pltpu.VMEM((1, turbines), f32),
            pltpu.VMEM((1, slots), jnp.int32),
            pltpu.VMEM((1, slots), jnp.int32),
            pltpu.VMEM((comps, width_x + 2, width_y, depth), f32),
            pltpu.VMEM(populations.shape, f32),
            pltpu.VMEM((fringe, n * chunk, depth), f32),
            pltpu.VMEM((fringe, n, chunk, depth), f32),
            pltpu.VMEM((fringe, n * chunk, depth), f32),
            pltpu.VMEM((n, BLOCK, LANES), f32),
            pltpu.VMEM((m, BLOCK, LANES), f32),
            pltpu.VMEM((BLOCK, LANES), f32),
            pltpu.VMEM((width_x, width_y, LANES), f32),
            pltpu.VMEM((2, width_x, 16, depth), f32),
            pltpu.VMEM((2, width_x + 2, 16, depth), f32),
            dma((fringe + 6,)), dma((width_x,)),
            dma((fringe * n,)), dma((fringe * n,)), dma((fringe * n,)), dma((fringe * n,)),
            dma((n,)), dma((n,)), dma((m,)), dma((m,)),
            dma((2,)), dma((2,)), dma((4,)), dma((4,)), dma((2,)), dma((2,)),
        ] + [pltpu.VMEM((n, chunk, depth), f32)] * fringe,
        compiler_params=pltpu.CompilerParams(
            collective_id=0, has_side_effects=True, vmem_limit_bytes=40 * 1024 * 1024),
    )(*(pltpu.with_memory_space_constraint(x, pltpu.HBM) for x in (
        populations, precursor, pairing, rates,
        loading.reshape(1, turbines), disc_cols.reshape(1, slots), disc_turb.reshape(1, slots),
    )))
    return out, speed.reshape(turbines)


def solution(mesh):
    n, m = mesh.shape["gx"], mesh.shape["gy"]
    in_specs = (P(None, "gx", "gy", None), P(None, "gx", "gy", None), P(), P(), P(), P(), P())
    out_specs = (P(None, "gx", "gy", None), P())
    return jax.shard_map(
        functools.partial(body, n, m), mesh=mesh, in_specs=in_specs, out_specs=out_specs, check_vma=False)
```

```python
import functools
import jax
import jax.numpy as jnp
import numpy as np
from jax import lax
from jax.experimental import pallas as pl
from jax.experimental.pallas import tpu as pltpu
from jax.sharding import PartitionSpec as P

MESH = pl.DeviceIdType.MESH
LANES = 128
BLOCK = 8
LOW = (0, 9, 3, 1, 18, 6, 2, 12, 10, 4)


def forward(cells):
    cells = list(cells)
    for stride in (9, 3, 1):
        for i in range(27):
            if (i // stride) % 3 == 0:
                low, mid, high = cells[i], cells[i + stride], cells[i + 2 * stride]
                even = (low + high) * (1.0 / 6.0)
                cells[i] = even + mid * (2.0 / 3.0)
                cells[i + stride] = (high - low) * (1.0 / 6.0)
                cells[i + 2 * stride] = even
    return cells


def backward(moments):
    cells = list(moments)
    for stride in (9, 3, 1):
        for i in range(27):
            if (i // stride) % 3 == 0:
                zero, one, two = cells[i], cells[i + stride], cells[i + 2 * stride]
                odd, even = one * 3.0, two * 3.0
                cells[i] = even - odd
                cells[i + stride] = (zero - two) * 1.5
                cells[i + 2 * stride] = even + odd
    return cells


def balance_moments(density, velocity):
    flux = [density * v for v in velocity]
    out = []
    for i in range(27):
        powers = (i // 9, (i // 3) % 3, i % 3)
        scale = (1.0 / 3.0) ** sum(p == 2 for p in powers)
        odd = [d for d in range(3) if powers[d] == 1]
        if len(odd) == 3:
            out.append(None)
            continue
        if len(odd) == 2:
            value = flux[odd[0]] * velocity[odd[1]]
        elif len(odd) == 1:
            value = flux[odd[0]]
        else:
            value = density
            for d in range(3):
                if powers[d] == 2:
                    value = value + 3.0 * (flux[d] * velocity[d])
        out.append(value if scale == 1.0 else value * scale)
    return out


def rebuild(low):
    rho, jx, jy, jz, xx, yy, zz, xy, xz, yz = low
    base = 2.5 * rho - 1.5 * (xx + yy + zz)
    third = rho * (1.0 / 3.0)
    linear = (3.0 * jx, 3.0 * jy, 3.0 * jz)
    square = (4.5 * (xx - third), 4.5 * (yy - third), 4.5 * (zz - third))
    cross = (9.0 * xy, 9.0 * xz, 9.0 * yz)

    def one(d, step):
        return square[d] + linear[d] if step > 0 else square[d] - linear[d]

    def signed(value, term, sign):
        return value + term if sign > 0 else value - term

    out = []
    for i in range(27):
        steps = (i // 9 - 1, (i // 3) % 3 - 1, i % 3 - 1)
        value = base
        for d in range(3):
            if steps[d]:
                value = value + one(d, steps[d])
        for (a, b), term in zip(((0, 1), (0, 2), (1, 2)), cross):
            if steps[a] * steps[b]:
                value = signed(value, term, steps[a] * steps[b])
        out.append(value)
    return out


def row_of(kx, kz):
    return kx * 3 + kz if kx < 2 else 8 + kz


def kernel(
    n, m, chunk,
    pops_hbm, prec_hbm, pairing_hbm, rates_hbm, loading_hbm, cols_hbm, turb_hbm,
    out_hbm, speed,
    pops, prec, pairing, rates, loading, cols, turb,
    post, outv, mom, stage, final, tot_x, tot_y, load_pad, hits, ysend, yrecv,
    in_sem, out_sem, a_send, a_recv, b_send, b_recv, tx_send, tx_recv, ty_send, ty_recv,
    x_send, x_recv, y_send, y_recv, c_send, c_recv, *got,
):
    comps, width_x, width_y, depth = pops.shape
    fringe = prec.shape[1]
    turbines = loading.shape[1]
    blocks = width_y // BLOCK
    me, my = lax.axis_index("gx"), lax.axis_index("gy")
    right, left = lax.rem(me + 1, n), lax.rem(me + n - 1, n)
    above, below = lax.rem(my + 1, m), lax.rem(my + m - 1, m)

    prec_in = [
        pltpu.make_async_copy(prec_hbm.at[:, p], prec.at[:, p], in_sem.at[p]) for p in range(fringe)]
    small_in = [
        pltpu.make_async_copy(source, target, in_sem.at[fringe + 1 + k])
        for k, (source, target) in enumerate((
            (cols_hbm, cols), (turb_hbm, turb), (pairing_hbm, pairing), (rates_hbm, rates),
            (loading_hbm, loading)))]
    pops_in = pltpu.make_async_copy(pops_hbm, pops, in_sem.at[fringe])
    for copy in prec_in + small_in + [pops_in]:
        copy.start()

    barrier = pltpu.get_barrier_semaphore()

    def greet_x(i, _):
        pl.semaphore_signal(barrier, inc=1, device_id={"gx": lax.rem(me + i, n)}, device_id_type=MESH)
        return 0

    def greet_y(i, _):
        pl.semaphore_signal(barrier, inc=1, device_id={"gy": lax.rem(my + i, m)}, device_id_type=MESH)
        return 0

    lax.fori_loop(1, n, greet_x, 0)
    lax.fori_loop(1, m, greet_y, 0)

    heights = lax.broadcasted_iota(jnp.int32, (BLOCK, depth), 1).astype(jnp.float32)
    profile = jnp.exp(-jnp.square((heights - depth / 3.0) / (depth / 6.0)))

    def span(j):
        return pl.ds(pl.multiple_of(j * chunk, BLOCK), chunk)

    def first(p, i, sent):
        other = lax.rem(me + i, n)
        slot = me if sent else other
        return pltpu.make_async_remote_copy(
            src_ref=mom.at[p, span(other), :], dst_ref=got[p].at[slot],
            send_sem=a_send.at[p * n + other], recv_sem=a_recv.at[p * n + slot],
            device_id={"gx": other}, device_id_type=MESH)

    def second(p, i, sent):
        other = lax.rem(me + i, n)
        slot = me if sent else other
        return pltpu.make_async_remote_copy(
            src_ref=stage.at[p, other], dst_ref=final.at[p, span(slot), :],
            send_sem=b_send.at[p * n + other], recv_sem=b_recv.at[p * n + slot],
            device_id={"gx": other}, device_id_type=MESH)

    def total_x(i, sent):
        other = lax.rem(me + i, n)
        slot = me if sent else other
        return pltpu.make_async_remote_copy(
            src_ref=tot_x.at[slot], dst_ref=tot_x.at[slot],
            send_sem=tx_send.at[other], recv_sem=tx_recv.at[slot],
            device_id={"gx": other}, device_id_type=MESH)

    def total_y(i, sent):
        other = lax.rem(my + i, m)
        slot = my if sent else other
        return pltpu.make_async_remote_copy(
            src_ref=tot_y.at[slot], dst_ref=tot_y.at[slot],
            send_sem=ty_send.at[other], recv_sem=ty_recv.at[slot],
            device_id={"gy": other}, device_id_type=MESH)

    def each(count, action):
        def step(i, _):
            action(i)
            return 0

        lax.fori_loop(1, count, step, 0)

    for p in range(fringe):
        prec_in[p].wait()

        def precursor_block(b, _, p=p):
            rows = pl.ds(pl.multiple_of(b * BLOCK, BLOCK), BLOCK)
            moments = forward([prec[i, p, rows, :] for i in range(27)])
            for q in range(10):
                start = pl.multiple_of(q * width_y + b * BLOCK, BLOCK)
                mom[p, pl.ds(start, BLOCK), :] = moments[LOW[q]]
            return 0

        lax.fori_loop(0, blocks, precursor_block, 0)
        if p == 0:
            pl.semaphore_wait(barrier, n + m - 2)
        each(n, lambda i, p=p: first(p, i, True).start())

    for copy in small_in:
        copy.wait()
    slots = cols.shape[1]
    owner = (
        lax.broadcasted_iota(jnp.int32, (LANES, slots), 0) == turb[...]
    ).astype(jnp.float32).astype(jnp.bfloat16)
    contract = (((1,), (1,)), ((), ()))
    counts = lax.dot_general(
        jnp.ones((BLOCK, slots), jnp.bfloat16), owner, contract, preferred_element_type=jnp.float32)
    shape = (width_x, width_y, slots)
    column = (
        (lax.broadcasted_iota(jnp.int32, shape, 0) + me * width_x) * (width_y * m)
        + lax.broadcasted_iota(jnp.int32, shape, 1) + my * width_y)
    match = (column == cols[...].reshape(1, 1, slots)).astype(jnp.float32).astype(jnp.bfloat16)
    hits[...] = lax.dot_general(
        match.reshape(width_x * width_y, slots), owner, contract, preferred_element_type=jnp.float32
    ).reshape(width_x, width_y, LANES)

    pops_in.wait()

    def share(x, acc):
        sheets = []
        for kx in range(3):
            c = [pops[9 * kx + k, x] for k in range(9)]
            corner = (c[0] + c[2]) + (c[6] + c[8])
            edge = (c[1] + c[3]) + (c[5] + c[7])
            sheets.append(corner * (1.0 / 36.0) + edge * (1.0 / 9.0) + c[4] * (4.0 / 9.0))
        density = (sheets[0] + sheets[2]) * (1.0 / 6.0) + sheets[1] * (2.0 / 3.0)
        velocity = (sheets[2] - sheets[0]) * (1.0 / 6.0) / density
        return acc + jnp.sum(velocity * profile[:1], axis=1, keepdims=True) * hits[x]

    acc = lax.fori_loop(0, width_x, share, jnp.zeros((width_y, LANES), jnp.float32))
    tot_x[me] = jnp.sum(acc, axis=0, keepdims=True)
    each(n, lambda i: total_x(i, True).start())

    def collide_block(x, b):
        rows = pl.ds(pl.multiple_of(b * BLOCK, BLOCK), BLOCK)
        moments = forward([pops[i, x, rows, :] for i in range(27)])
        density = moments[0]
        inverse = 1.0 / density
        velocity = [moments[9] * inverse, moments[3] * inverse, moments[1] * inverse]
        balance = balance_moments(density, velocity)
        relaxed = []
        for i in range(27):
            gap = moments[i] if balance[i] is None else moments[i] - balance[i]
            relaxed.append(moments[i] - rates[i] * gap)
        for i, value in enumerate(backward(relaxed)):
            post[i, x + 1, rows, :] = value

    def collide(start, stop):
        def step(k, _):
            collide_block(k // blocks, k % blocks)
            return 0

        lax.fori_loop(start * blocks, stop * blocks, step, 0)

    def pass_on(p):
        got[p][me] = mom[p, span(me), :]
        each(n, lambda i: first(p, i, False).wait_recv())

        def forward_chunk(i, _):
            to = lax.rem(me + i, n)
            stage[p, to] = got[p][pairing[to]]
            second(p, i, True).start()
            return 0

        lax.fori_loop(1, n, forward_chunk, 0)
        final[p, span(me), :] = got[p][pairing[me]]

    part = -(-width_x // (fringe + 1))
    for p in range(fringe):
        collide(p * part, (p + 1) * part)
        pass_on(p)

    each(n, lambda i: total_x(i, False).wait_recv())
    tot_y[my] = lax.fori_loop(1, n, lambda i, t: t + tot_x[i], tot_x[0])
    each(m, lambda i: total_y(i, True).start())
    collide(fringe * part, width_x)

    load_pad[...] = jnp.zeros((BLOCK, LANES), jnp.float32)
    load_pad[:, :turbines] = jnp.broadcast_to(loading[...], (BLOCK, turbines))
    norm = counts * jnp.sum(profile, axis=1, keepdims=True)
    each(m, lambda i: total_y(i, False).wait_recv())
    totals = lax.fori_loop(1, m, lambda i, t: t + tot_y[i], tot_y[0])
    disc_speed = totals / jnp.where(counts > 0.0, norm, 1.0)[:1]
    speed[...] = disc_speed[:, :turbines]
    thrust = 0.5 * load_pad[:1] * disc_speed * jnp.abs(disc_speed)

    def push(x, _):
        column = jnp.sum(hits[x] * thrust, axis=1, keepdims=True)
        kick = (-3.0 * column) * profile[:1]
        for i in range(9):
            post[i, x + 1] = post[i, x + 1] - kick
        for i in range(18, 27):
            post[i, x + 1] = post[i, x + 1] + kick
        return 0

    lax.fori_loop(0, width_x, push, 0)

    def x_copy(way):
        if way:
            src, dst, to = post.at[pl.ds(18, 9), width_x], post.at[pl.ds(18, 9), 0], right
        else:
            src, dst, to = post.at[pl.ds(0, 9), 1], post.at[pl.ds(0, 9), width_x + 1], left
        return pltpu.make_async_remote_copy(
            src_ref=src, dst_ref=dst, send_sem=x_send.at[way], recv_sem=x_recv.at[way],
            device_id={"gx": to}, device_id_type=MESH)

    def y_copy(way, late):
        planes = (late - 1, 1) if late else (fringe, width_x - fringe)
        return pltpu.make_async_remote_copy(
            src_ref=ysend.at[way, pl.ds(planes[0], planes[1])],
            dst_ref=yrecv.at[way, pl.ds(planes[0] + 1, planes[1])],
            send_sem=y_send.at[(fringe + 1) * way + late], recv_sem=y_recv.at[(fringe + 1) * way + late],
            device_id={"gy": above if way else below}, device_id_type=MESH)

    def corner_copy(way):
        if way:
            src, dst, to = yrecv.at[:, width_x, pl.ds(8, 8)], yrecv.at[:, 0, pl.ds(8, 8)], right
        else:
            src, dst, to = yrecv.at[:, 1, pl.ds(0, 8)], yrecv.at[:, width_x + 1, pl.ds(0, 8)], left
        return pltpu.make_async_remote_copy(
            src_ref=src, dst_ref=dst, send_sem=c_send.at[way], recv_sem=c_recv.at[way],
            device_id={"gx": to}, device_id_type=MESH)

    def pack(x, _):
        for way in range(2):
            edge = width_y - 1 if way else 0
            for kx in range(3):
                for kz in range(3):
                    row = row_of(kx, kz)
                    ysend[way, x, row : row + 1, :] = post[
                        9 * kx + 6 * way + kz, x + 1, edge : edge + 1, :]
        return 0

    lane = lax.broadcasted_iota(jnp.int32, (width_y, depth), 1)
    sub = lax.broadcasted_iota(jnp.int32, (width_y, depth), 0)

    def out_copy(x):
        return pltpu.make_async_copy(outv.at[:, x], out_hbm.at[:, x], out_sem.at[x])

    def stream(x, _):
        for i in range(27):
            kx, ky, kz = i // 9, (i // 3) % 3, i % 3
            source = x + 2 - kx
            moved = post[i, source]
            if ky != 1:
                way = 1 if ky == 2 else 0
                row = row_of(kx, kz)
                halo = yrecv[way, source, row : row + 1, :]
                moved = pltpu.roll(moved, 1 if way else width_y - 1, 0)
                moved = jnp.where(sub == (0 if way else width_y - 1), halo, moved)
            if kz != 1:
                moved = pltpu.roll(moved, 1 if kz == 2 else depth - 1, 1)
                moved = jnp.where(lane == (0 if kz == 2 else depth - 1), post[26 - i, x + 1], moved)
            outv[i, x] = moved
        out_copy(x).start()
        return 0

    x_copy(1).start()
    lax.fori_loop(fringe, width_x, pack, 0)
    for way in range(2):
        y_copy(way, 0).start()

    for p in range(fringe):
        blend = 0.5 / (p + 1.0)
        each(n, lambda i, p=p: second(p, i, False).wait_recv())

        def blend_block(b, _, p=p, blend=blend):
            rows = pl.ds(pl.multiple_of(b * BLOCK, BLOCK), BLOCK)
            low = []
            for q in range(10):
                start = pl.multiple_of(q * width_y + b * BLOCK, BLOCK)
                low.append(final[p, pl.ds(start, BLOCK), :])
            for i, value in enumerate(rebuild(low)):
                post[i, p + 1, rows, :] = (1.0 - blend) * post[i, p + 1, rows, :] + blend * value
            return 0

        lax.fori_loop(0, blocks, blend_block, 0)
        if p == 0:
            x_copy(0).start()
        pack(p, 0)
        for way in range(2):
            y_copy(way, p + 1).start()
        if p == 0:
            for way in range(2):
                y_copy(way, 0).wait_recv()
            corner_copy(1).start()
            lax.fori_loop(fringe + 1, width_x - 1, stream, 0)
            for way in range(2):
                y_copy(way, 1).wait_recv()
            corner_copy(0).start()

    for late in range(2, fringe + 1):
        for way in range(2):
            y_copy(way, late).wait_recv()
    x_copy(1).wait_recv()
    corner_copy(1).wait_recv()
    lax.fori_loop(0, fringe + 1, stream, 0)
    x_copy(0).wait_recv()
    corner_copy(0).wait_recv()
    lax.fori_loop(width_x - 1, width_x, stream, 0)

    for p in range(fringe):
        each(n, lambda i, p=p: first(p, i, True).wait_send())
        each(n, lambda i, p=p: second(p, i, True).wait_send())
    each(n, lambda i: total_x(i, True).wait_send())
    each(m, lambda i: total_y(i, True).wait_send())
    for way in range(2):
        x_copy(way).wait_send()
        corner_copy(way).wait_send()
        for late in range(fringe + 1):
            y_copy(way, late).wait_send()

    def drain(x, _):
        out_copy(x).wait()
        return 0

    lax.fori_loop(0, width_x, drain, 0)


def body(n, m, populations, precursor, pairing, rates, loading, disc_cols, disc_turb):
    comps, width_x, width_y, depth = populations.shape
    fringe = precursor.shape[1]
    rows = 10 * width_y
    chunk = -(-rows // (n * BLOCK)) * BLOCK
    turbines = loading.shape[0]
    slots = disc_cols.shape[0]
    f32 = jnp.float32
    anywhere = pl.BlockSpec(memory_space=pl.ANY)
    hbm = pl.BlockSpec(memory_space=pltpu.HBM)
    vmem = pl.BlockSpec(memory_space=pltpu.VMEM)
    dma = pltpu.SemaphoreType.DMA
    out, speed = pl.pallas_call(
        functools.partial(kernel, n, m, chunk),
        out_shape=(
            pltpu.VMEM(populations.shape, f32),
            jax.ShapeDtypeStruct((1, turbines), f32),
        ),
        in_specs=[hbm] * 7,
        out_specs=(anywhere, vmem),
        scratch_shapes=[
            pltpu.VMEM(populations.shape, f32),
            pltpu.VMEM(precursor.shape, f32),
            pltpu.SMEM(pairing.shape, jnp.int32),
            pltpu.SMEM(rates.shape, f32),
            pltpu.VMEM((1, turbines), f32),
            pltpu.VMEM((1, slots), jnp.int32),
            pltpu.VMEM((1, slots), jnp.int32),
            pltpu.VMEM((comps, width_x + 2, width_y, depth), f32),
            pltpu.VMEM(populations.shape, f32),
            pltpu.VMEM((fringe, n * chunk, depth), f32),
            pltpu.VMEM((fringe, n, chunk, depth), f32),
            pltpu.VMEM((fringe, n * chunk, depth), f32),
            pltpu.VMEM((n, 1, LANES), f32),
            pltpu.VMEM((m, 1, LANES), f32),
            pltpu.VMEM((BLOCK, LANES), f32),
            pltpu.VMEM((width_x, width_y, LANES), f32),
            pltpu.VMEM((2, width_x, 16, depth), f32),
            pltpu.VMEM((2, width_x + 2, 16, depth), f32),
            dma((fringe + 6,)), dma((width_x,)),
            dma((fringe * n,)), dma((fringe * n,)), dma((fringe * n,)), dma((fringe * n,)),
            dma((n,)), dma((n,)), dma((m,)), dma((m,)),
            dma((2,)), dma((2,)), dma((2 * fringe + 2,)), dma((2 * fringe + 2,)), dma((2,)), dma((2,)),
        ] + [pltpu.VMEM((n, chunk, depth), f32)] * fringe,
        compiler_params=pltpu.CompilerParams(
            collective_id=0, has_side_effects=True, vmem_limit_bytes=40 * 1024 * 1024),
    )(*(pltpu.with_memory_space_constraint(x, pltpu.HBM) for x in (
        populations, precursor, pairing, rates,
        loading.reshape(1, turbines), disc_cols.reshape(1, slots), disc_turb.reshape(1, slots),
    )))
    return out, speed.reshape(turbines)


def solution(mesh):
    n, m = mesh.shape["gx"], mesh.shape["gy"]
    in_specs = (P(None, "gx", "gy", None), P(None, "gx", "gy", None), P(), P(), P(), P(), P())
    out_specs = (P(None, "gx", "gy", None), P())
    return jax.shard_map(
        functools.partial(body, n, m), mesh=mesh, in_specs=in_specs, out_specs=out_specs, check_vma=False)
```

```python
import functools
import jax
import jax.numpy as jnp
import numpy as np
from jax import lax
from jax.experimental import pallas as pl
from jax.experimental.pallas import tpu as pltpu
from jax.sharding import PartitionSpec as P

MESH = pl.DeviceIdType.MESH
LANES = 128
BLOCK = 8
LOW = (0, 9, 3, 1, 18, 6, 2, 12, 10, 4)


def forward(cells):
    cells = list(cells)
    for stride in (9, 3, 1):
        for i in range(27):
            if (i // stride) % 3 == 0:
                low, mid, high = cells[i], cells[i + stride], cells[i + 2 * stride]
                even = (low + high) * (1.0 / 6.0)
                cells[i] = even + mid * (2.0 / 3.0)
                cells[i + stride] = (high - low) * (1.0 / 6.0)
                cells[i + 2 * stride] = even
    return cells


def backward(moments):
    cells = list(moments)
    for stride in (9, 3, 1):
        for i in range(27):
            if (i // stride) % 3 == 0:
                zero, one, two = cells[i], cells[i + stride], cells[i + 2 * stride]
                odd, even = one * 3.0, two * 3.0
                cells[i] = even - odd
                cells[i + stride] = (zero - two) * 1.5
                cells[i + 2 * stride] = even + odd
    return cells


def balance_moments(density, velocity):
    flux = [density * v for v in velocity]
    out = []
    for i in range(27):
        powers = (i // 9, (i // 3) % 3, i % 3)
        scale = (1.0 / 3.0) ** sum(p == 2 for p in powers)
        odd = [d for d in range(3) if powers[d] == 1]
        if len(odd) == 3:
            out.append(None)
            continue
        if len(odd) == 2:
            value = flux[odd[0]] * velocity[odd[1]]
        elif len(odd) == 1:
            value = flux[odd[0]]
        else:
            value = density
            for d in range(3):
                if powers[d] == 2:
                    value = value + 3.0 * (flux[d] * velocity[d])
        out.append(value if scale == 1.0 else value * scale)
    return out


def rebuild(low):
    rho, jx, jy, jz, xx, yy, zz, xy, xz, yz = low
    base = 2.5 * rho - 1.5 * (xx + yy + zz)
    third = rho * (1.0 / 3.0)
    linear = (3.0 * jx, 3.0 * jy, 3.0 * jz)
    square = (4.5 * (xx - third), 4.5 * (yy - third), 4.5 * (zz - third))
    cross = (9.0 * xy, 9.0 * xz, 9.0 * yz)

    def one(d, step):
        return square[d] + linear[d] if step > 0 else square[d] - linear[d]

    def signed(value, term, sign):
        return value + term if sign > 0 else value - term

    out = []
    for i in range(27):
        steps = (i // 9 - 1, (i // 3) % 3 - 1, i % 3 - 1)
        value = base
        for d in range(3):
            if steps[d]:
                value = value + one(d, steps[d])
        for (a, b), term in zip(((0, 1), (0, 2), (1, 2)), cross):
            if steps[a] * steps[b]:
                value = signed(value, term, steps[a] * steps[b])
        out.append(value)
    return out


def row_of(kx, kz):
    return kx * 3 + kz if kx < 2 else 8 + kz


def kernel(
    n, m, chunk,
    pops_hbm, prec_hbm, pairing_hbm, rates_hbm, loading_hbm, cols_hbm, turb_hbm,
    out_hbm, speed,
    pops, prec, pairing, rates, loading, cols, turb,
    post, outv, mom, stage, final, tot_x, tot_y, load_pad, hits, ysend, yrecv,
    in_sem, out_sem, a_send, a_recv, b_send, b_recv, tx_send, tx_recv, ty_send, ty_recv,
    x_send, x_recv, y_send, y_recv, c_send, c_recv, *got,
):
    comps, width_x, width_y, depth = pops.shape
    fringe = prec.shape[1]
    turbines = loading.shape[1]
    blocks = width_y // BLOCK
    me, my = lax.axis_index("gx"), lax.axis_index("gy")
    right, left = lax.rem(me + 1, n), lax.rem(me + n - 1, n)
    above, below = lax.rem(my + 1, m), lax.rem(my + m - 1, m)

    prec_in = [
        pltpu.make_async_copy(prec_hbm.at[:, p], prec.at[:, p], in_sem.at[p]) for p in range(fringe)]
    small_in = [
        pltpu.make_async_copy(source, target, in_sem.at[fringe + 1 + k])
        for k, (source, target) in enumerate((
            (cols_hbm, cols), (turb_hbm, turb), (pairing_hbm, pairing), (rates_hbm, rates),
            (loading_hbm, loading)))]
    pops_in = pltpu.make_async_copy(pops_hbm, pops, in_sem.at[fringe])
    for copy in prec_in + small_in + [pops_in]:
        copy.start()

    barrier = pltpu.get_barrier_semaphore()

    def greet_x(i, _):
        pl.semaphore_signal(barrier, inc=1, device_id={"gx": lax.rem(me + i, n)}, device_id_type=MESH)
        return 0

    def greet_y(i, _):
        pl.semaphore_signal(barrier, inc=1, device_id={"gy": lax.rem(my + i, m)}, device_id_type=MESH)
        return 0

    lax.fori_loop(1, n, greet_x, 0)
    lax.fori_loop(1, m, greet_y, 0)

    heights = lax.broadcasted_iota(jnp.int32, (BLOCK, depth), 1).astype(jnp.float32)
    profile = jnp.exp(-jnp.square((heights - depth / 3.0) / (depth / 6.0)))

    def span(j):
        return pl.ds(pl.multiple_of(j * chunk, BLOCK), chunk)

    def first(p, i, sent):
        other = lax.rem(me + i, n)
        slot = me if sent else other
        return pltpu.make_async_remote_copy(
            src_ref=mom.at[p, span(other), :], dst_ref=got[p].at[slot],
            send_sem=a_send.at[p * n + other], recv_sem=a_recv.at[p * n + slot],
            device_id={"gx": other}, device_id_type=MESH)

    def second(p, i, sent):
        other = lax.rem(me + i, n)
        slot = me if sent else other
        return pltpu.make_async_remote_copy(
            src_ref=stage.at[p, other], dst_ref=final.at[p, span(slot), :],
            send_sem=b_send.at[p * n + other], recv_sem=b_recv.at[p * n + slot],
            device_id={"gx": other}, device_id_type=MESH)

    def total_x(i, sent):
        other = lax.rem(me + i, n)
        slot = me if sent else other
        return pltpu.make_async_remote_copy(
            src_ref=tot_x.at[slot], dst_ref=tot_x.at[slot],
            send_sem=tx_send.at[other], recv_sem=tx_recv.at[slot],
            device_id={"gx": other}, device_id_type=MESH)

    def total_y(i, sent):
        other = lax.rem(my + i, m)
        slot = my if sent else other
        return pltpu.make_async_remote_copy(
            src_ref=tot_y.at[slot], dst_ref=tot_y.at[slot],
            send_sem=ty_send.at[other], recv_sem=ty_recv.at[slot],
            device_id={"gy": other}, device_id_type=MESH)

    def each(count, action):
        def step(i, _):
            action(i)
            return 0

        lax.fori_loop(1, count, step, 0)

    for p in range(fringe):
        prec_in[p].wait()

        def precursor_block(b, _, p=p):
            rows = pl.ds(pl.multiple_of(b * BLOCK, BLOCK), BLOCK)
            moments = forward([prec[i, p, rows, :] for i in range(27)])
            for q in range(10):
                start = pl.multiple_of(q * width_y + b * BLOCK, BLOCK)
                mom[p, pl.ds(start, BLOCK), :] = moments[LOW[q]]
            return 0

        lax.fori_loop(0, blocks, precursor_block, 0)
        if p == 0:
            pl.semaphore_wait(barrier, n + m - 2)
        each(n, lambda i, p=p: first(p, i, True).start())

    for copy in small_in:
        copy.wait()
    slots = cols.shape[1]
    owner = (
        lax.broadcasted_iota(jnp.int32, (LANES, slots), 0) == turb[...]
    ).astype(jnp.float32).astype(jnp.bfloat16)
    contract = (((1,), (1,)), ((), ()))
    counts = lax.dot_general(
        jnp.ones((BLOCK, slots), jnp.bfloat16), owner, contract, preferred_element_type=jnp.float32)
    shape = (width_x, width_y, slots)
    column = (
        (lax.broadcasted_iota(jnp.int32, shape, 0) + me * width_x) * (width_y * m)
        + lax.broadcasted_iota(jnp.int32, shape, 1) + my * width_y)
    match = (column == cols[...].reshape(1, 1, slots)).astype(jnp.float32).astype(jnp.bfloat16)
    hits[...] = lax.dot_general(
        match.reshape(width_x * width_y, slots), owner, contract, preferred_element_type=jnp.float32
    ).reshape(width_x, width_y, LANES)

    pops_in.wait()

    def share(x, acc):
        sheets = []
        for kx in range(3):
            c = [pops[9 * kx + k, x] for k in range(9)]
            corner = (c[0] + c[2]) + (c[6] + c[8])
            edge = (c[1] + c[3]) + (c[5] + c[7])
            sheets.append(corner * (1.0 / 36.0) + edge * (1.0 / 9.0) + c[4] * (4.0 / 9.0))
        density = (sheets[0] + sheets[2]) * (1.0 / 6.0) + sheets[1] * (2.0 / 3.0)
        velocity = (sheets[2] - sheets[0]) * (1.0 / 6.0) / density
        return acc + jnp.sum(velocity * profile[:1], axis=1, keepdims=True) * hits[x]

    acc = lax.fori_loop(0, width_x, share, jnp.zeros((width_y, LANES), jnp.float32))
    tot_x[me] = jnp.sum(acc, axis=0, keepdims=True)
    each(n, lambda i: total_x(i, True).start())

    def collide_block(x, b):
        rows = pl.ds(pl.multiple_of(b * BLOCK, BLOCK), BLOCK)
        moments = forward([pops[i, x, rows, :] for i in range(27)])
        density = moments[0]
        inverse = 1.0 / density
        velocity = [moments[9] * inverse, moments[3] * inverse, moments[1] * inverse]
        balance = balance_moments(density, velocity)
        relaxed = []
        for i in range(27):
            gap = moments[i] if balance[i] is None else moments[i] - balance[i]
            relaxed.append(moments[i] - rates[i] * gap)
        for i, value in enumerate(backward(relaxed)):
            post[i, x + 1, rows, :] = value

    def collide(start, stop):
        def step(k, _):
            collide_block(k // blocks, k % blocks)
            return 0

        lax.fori_loop(start * blocks, stop * blocks, step, 0)

    def pass_on(p):
        got[p][me] = mom[p, span(me), :]
        each(n, lambda i: first(p, i, False).wait_recv())

        def forward_chunk(i, _):
            to = lax.rem(me + i, n)
            stage[p, to] = got[p][pairing[to]]
            second(p, i, True).start()
            return 0

        lax.fori_loop(1, n, forward_chunk, 0)
        final[p, span(me), :] = got[p][pairing[me]]

    part = -(-width_x // (fringe + 1))
    for p in range(fringe):
        collide(p * part, (p + 1) * part)
        pass_on(p)

    each(n, lambda i: total_x(i, False).wait_recv())
    tot_y[my] = lax.fori_loop(1, n, lambda i, t: t + tot_x[i], tot_x[0])
    each(m, lambda i: total_y(i, True).start())
    collide(fringe * part, width_x)

    load_pad[...] = jnp.zeros((BLOCK, LANES), jnp.float32)
    load_pad[:, :turbines] = jnp.broadcast_to(loading[...], (BLOCK, turbines))
    norm = counts * jnp.sum(profile, axis=1, keepdims=True)
    each(m, lambda i: total_y(i, False).wait_recv())
    totals = lax.fori_loop(1, m, lambda i, t: t + tot_y[i], tot_y[0])
    disc_speed = totals / jnp.where(counts > 0.0, norm, 1.0)[:1]
    speed[...] = disc_speed[:, :turbines]
    thrust = 0.5 * load_pad[:1] * disc_speed * jnp.abs(disc_speed)

    def push(x, _):
        column = jnp.sum(hits[x] * thrust, axis=1, keepdims=True)
        kick = (-3.0 * column) * profile[:1]
        for i in range(9):
            post[i, x + 1] = post[i, x + 1] - kick
        for i in range(18, 27):
            post[i, x + 1] = post[i, x + 1] + kick
        return 0

    lax.fori_loop(0, width_x, push, 0)

    def x_copy(way):
        if way:
            src, dst, to = post.at[pl.ds(18, 9), width_x], post.at[pl.ds(18, 9), 0], right
        else:
            src, dst, to = post.at[pl.ds(0, 9), 1], post.at[pl.ds(0, 9), width_x + 1], left
        return pltpu.make_async_remote_copy(
            src_ref=src, dst_ref=dst, send_sem=x_send.at[way], recv_sem=x_recv.at[way],
            device_id={"gx": to}, device_id_type=MESH)

    def y_copy(way, late):
        planes = (late - 1, 1) if late else (fringe, width_x - fringe)
        return pltpu.make_async_remote_copy(
            src_ref=ysend.at[way, pl.ds(planes[0], planes[1])],
            dst_ref=yrecv.at[way, pl.ds(planes[0] + 1, planes[1])],
            send_sem=y_send.at[(fringe + 1) * way + late], recv_sem=y_recv.at[(fringe + 1) * way + late],
            device_id={"gy": above if way else below}, device_id_type=MESH)

    def corner_copy(way):
        if way:
            src, dst, to = yrecv.at[:, width_x, pl.ds(8, 8)], yrecv.at[:, 0, pl.ds(8, 8)], right
        else:
            src, dst, to = yrecv.at[:, 1, pl.ds(0, 8)], yrecv.at[:, width_x + 1, pl.ds(0, 8)], left
        return pltpu.make_async_remote_copy(
            src_ref=src, dst_ref=dst, send_sem=c_send.at[way], recv_sem=c_recv.at[way],
            device_id={"gx": to}, device_id_type=MESH)

    def pack(x, _):
        for way in range(2):
            edge = width_y - 1 if way else 0
            for kx in range(3):
                for kz in range(3):
                    row = row_of(kx, kz)
                    ysend[way, x, row : row + 1, :] = post[
                        9 * kx + 6 * way + kz, x + 1, edge : edge + 1, :]
        return 0

    lane = lax.broadcasted_iota(jnp.int32, (width_y, depth), 1)
    sub = lax.broadcasted_iota(jnp.int32, (width_y, depth), 0)

    def out_copy(x):
        return pltpu.make_async_copy(outv.at[:, x], out_hbm.at[:, x], out_sem.at[x])

    def stream(x, _):
        for i in range(27):
            kx, ky, kz = i // 9, (i // 3) % 3, i % 3
            source = x + 2 - kx
            moved = post[i, source]
            if ky != 1:
                way = 1 if ky == 2 else 0
                row = row_of(kx, kz)
                halo = yrecv[way, source, row : row + 1, :]
                moved = pltpu.roll(moved, 1 if way else width_y - 1, 0)
                moved = jnp.where(sub == (0 if way else width_y - 1), halo, moved)
            if kz != 1:
                moved = pltpu.roll(moved, 1 if kz == 2 else depth - 1, 1)
                moved = jnp.where(lane == (0 if kz == 2 else depth - 1), post[26 - i, x + 1], moved)
            outv[i, x] = moved
        out_copy(x).start()
        return 0

    x_copy(1).start()
    lax.fori_loop(fringe, width_x, pack, 0)
    for way in range(2):
        y_copy(way, 0).start()

    for p in range(fringe):
        blend = 0.5 / (p + 1.0)
        each(n, lambda i, p=p: second(p, i, False).wait_recv())

        def blend_block(b, _, p=p, blend=blend):
            rows = pl.ds(pl.multiple_of(b * BLOCK, BLOCK), BLOCK)
            low = []
            for q in range(10):
                start = pl.multiple_of(q * width_y + b * BLOCK, BLOCK)
                low.append(final[p, pl.ds(start, BLOCK), :])
            for i, value in enumerate(rebuild(low)):
                post[i, p + 1, rows, :] = (1.0 - blend) * post[i, p + 1, rows, :] + blend * value
            return 0

        lax.fori_loop(0, blocks, blend_block, 0)
        if p == 0:
            x_copy(0).start()
        pack(p, 0)
        for way in range(2):
            y_copy(way, p + 1).start()
        if p == 0:
            for way in range(2):
                y_copy(way, 0).wait_recv()
            corner_copy(1).start()
            lax.fori_loop(fringe + 1, width_x - 1, stream, 0)
            for way in range(2):
                y_copy(way, 1).wait_recv()
            corner_copy(0).start()

    for late in range(2, fringe + 1):
        for way in range(2):
            y_copy(way, late).wait_recv()
    x_copy(1).wait_recv()
    corner_copy(1).wait_recv()
    lax.fori_loop(0, fringe + 1, stream, 0)
    x_copy(0).wait_recv()
    corner_copy(0).wait_recv()
    lax.fori_loop(width_x - 1, width_x, stream, 0)

    for p in range(fringe):
        each(n, lambda i, p=p: first(p, i, True).wait_send())
        each(n, lambda i, p=p: second(p, i, True).wait_send())
    each(n, lambda i: total_x(i, True).wait_send())
    each(m, lambda i: total_y(i, True).wait_send())
    for way in range(2):
        x_copy(way).wait_send()
        corner_copy(way).wait_send()
        for late in range(fringe + 1):
            y_copy(way, late).wait_send()

    def drain(x, _):
        out_copy(x).wait()
        return 0

    lax.fori_loop(0, width_x, drain, 0)


def deliver_kernel(out_from, speed_from, out_to, speed_to, sems):
    count = out_from.shape[0]

    def copy(i):
        return pltpu.make_async_copy(out_from.at[i], out_to.at[i], sems.at[i])

    copies = [copy(i) for i in range(count)]
    copies.append(pltpu.make_async_copy(speed_from, speed_to, sems.at[count]))
    for item in copies:
        item.start()
    for item in copies:
        item.wait()


def deliver(out, speed, turbines):
    anywhere = pl.BlockSpec(memory_space=pl.ANY)
    vmem = pltpu.VMEM
    out, speed = pl.pallas_call(
        deliver_kernel,
        out_shape=(pltpu.HBM(out.shape, out.dtype), pltpu.HBM(speed.shape, speed.dtype)),
        in_specs=[anywhere, anywhere],
        out_specs=(anywhere, anywhere),
        scratch_shapes=[pltpu.SemaphoreType.DMA((out.shape[0] + 1,))],
    )(pltpu.with_memory_space_constraint(out, vmem), pltpu.with_memory_space_constraint(speed, vmem))
    return out, speed.reshape(turbines)


def body(n, m, populations, precursor, pairing, rates, loading, disc_cols, disc_turb):
    comps, width_x, width_y, depth = populations.shape
    fringe = precursor.shape[1]
    rows = 10 * width_y
    chunk = -(-rows // (n * BLOCK)) * BLOCK
    turbines = loading.shape[0]
    slots = disc_cols.shape[0]
    f32 = jnp.float32
    anywhere = pl.BlockSpec(memory_space=pl.ANY)
    hbm = pl.BlockSpec(memory_space=pltpu.HBM)
    vmem = pl.BlockSpec(memory_space=pltpu.VMEM)
    dma = pltpu.SemaphoreType.DMA
    out, speed = pl.pallas_call(
        functools.partial(kernel, n, m, chunk),
        out_shape=(
            pltpu.VMEM(populations.shape, f32),
            pltpu.VMEM((1, turbines), f32),
        ),
        in_specs=[hbm] * 7,
        out_specs=(anywhere, vmem),
        scratch_shapes=[
            pltpu.VMEM(populations.shape, f32),
            pltpu.VMEM(precursor.shape, f32),
            pltpu.SMEM(pairing.shape, jnp.int32),
            pltpu.SMEM(rates.shape, f32),
            pltpu.VMEM((1, turbines), f32),
            pltpu.VMEM((1, slots), jnp.int32),
            pltpu.VMEM((1, slots), jnp.int32),
            pltpu.VMEM((comps, width_x + 2, width_y, depth), f32),
            pltpu.VMEM(populations.shape, f32),
            pltpu.VMEM((fringe, n * chunk, depth), f32),
            pltpu.VMEM((fringe, n, chunk, depth), f32),
            pltpu.VMEM((fringe, n * chunk, depth), f32),
            pltpu.VMEM((n, 1, LANES), f32),
            pltpu.VMEM((m, 1, LANES), f32),
            pltpu.VMEM((BLOCK, LANES), f32),
            pltpu.VMEM((width_x, width_y, LANES), f32),
            pltpu.VMEM((2, width_x, 16, depth), f32),
            pltpu.VMEM((2, width_x + 2, 16, depth), f32),
            dma((fringe + 6,)), dma((width_x,)),
            dma((fringe * n,)), dma((fringe * n,)), dma((fringe * n,)), dma((fringe * n,)),
            dma((n,)), dma((n,)), dma((m,)), dma((m,)),
            dma((2,)), dma((2,)), dma((2 * fringe + 2,)), dma((2 * fringe + 2,)), dma((2,)), dma((2,)),
        ] + [pltpu.VMEM((n, chunk, depth), f32)] * fringe,
        compiler_params=pltpu.CompilerParams(
            collective_id=0, has_side_effects=True, vmem_limit_bytes=40 * 1024 * 1024),
    )(*(pltpu.with_memory_space_constraint(x, pltpu.HBM) for x in (
        populations, precursor, pairing, rates,
        loading.reshape(1, turbines), disc_cols.reshape(1, slots), disc_turb.reshape(1, slots),
    )))
    return deliver(out, speed, turbines)


def solution(mesh):
    n, m = mesh.shape["gx"], mesh.shape["gy"]
    in_specs = (P(None, "gx", "gy", None), P(None, "gx", "gy", None), P(), P(), P(), P(), P())
    out_specs = (P(None, "gx", "gy", None), P())
    return jax.shard_map(
        functools.partial(body, n, m), mesh=mesh, in_specs=in_specs, out_specs=out_specs, check_vma=False)
```

```python
import functools
import jax
import jax.numpy as jnp
import numpy as np
from jax import lax
from jax.experimental import pallas as pl
from jax.experimental.pallas import tpu as pltpu
from jax.sharding import PartitionSpec as P

MESH = pl.DeviceIdType.MESH
LANES = 128
BLOCK = 8
LOW = (0, 9, 3, 1, 18, 6, 2, 12, 10, 4)


def forward(cells):
    cells = list(cells)
    for stride in (9, 3, 1):
        for i in range(27):
            if (i // stride) % 3 == 0:
                low, mid, high = cells[i], cells[i + stride], cells[i + 2 * stride]
                even = (low + high) * (1.0 / 6.0)
                cells[i] = even + mid * (2.0 / 3.0)
                cells[i + stride] = (high - low) * (1.0 / 6.0)
                cells[i + 2 * stride] = even
    return cells


def backward(moments):
    cells = list(moments)
    for stride in (9, 3, 1):
        for i in range(27):
            if (i // stride) % 3 == 0:
                zero, one, two = cells[i], cells[i + stride], cells[i + 2 * stride]
                odd, even = one * 3.0, two * 3.0
                cells[i] = even - odd
                cells[i + stride] = (zero - two) * 1.5
                cells[i + 2 * stride] = even + odd
    return cells


def balance_moments(density, velocity):
    flux = [density * v for v in velocity]
    out = []
    for i in range(27):
        powers = (i // 9, (i // 3) % 3, i % 3)
        scale = (1.0 / 3.0) ** sum(p == 2 for p in powers)
        odd = [d for d in range(3) if powers[d] == 1]
        if len(odd) == 3:
            out.append(None)
            continue
        if len(odd) == 2:
            value = flux[odd[0]] * velocity[odd[1]]
        elif len(odd) == 1:
            value = flux[odd[0]]
        else:
            value = density
            for d in range(3):
                if powers[d] == 2:
                    value = value + 3.0 * (flux[d] * velocity[d])
        out.append(value if scale == 1.0 else value * scale)
    return out


def rebuild(low):
    rho, jx, jy, jz, xx, yy, zz, xy, xz, yz = low
    base = 2.5 * rho - 1.5 * (xx + yy + zz)
    third = rho * (1.0 / 3.0)
    linear = (3.0 * jx, 3.0 * jy, 3.0 * jz)
    square = (4.5 * (xx - third), 4.5 * (yy - third), 4.5 * (zz - third))
    cross = (9.0 * xy, 9.0 * xz, 9.0 * yz)

    def one(d, step):
        return square[d] + linear[d] if step > 0 else square[d] - linear[d]

    def signed(value, term, sign):
        return value + term if sign > 0 else value - term

    out = []
    for i in range(27):
        steps = (i // 9 - 1, (i // 3) % 3 - 1, i % 3 - 1)
        value = base
        for d in range(3):
            if steps[d]:
                value = value + one(d, steps[d])
        for (a, b), term in zip(((0, 1), (0, 2), (1, 2)), cross):
            if steps[a] * steps[b]:
                value = signed(value, term, steps[a] * steps[b])
        out.append(value)
    return out


def row_of(kx, kz):
    return kx * 3 + kz if kx < 2 else 8 + kz


def kernel(
    n, m, chunk,
    pops_hbm, prec_hbm, pairing_hbm, rates_hbm, loading_hbm, cols_hbm, turb_hbm,
    out_hbm, speed,
    pops, prec, pairing, rates, loading, cols, turb,
    post, outv, mom, stage, final, tot_x, tot_y, load_pad, hits, ysend, yrecv,
    in_sem, out_sem, a_send, a_recv, b_send, b_recv, tx_send, tx_recv, ty_send, ty_recv,
    x_send, x_recv, y_send, y_recv, c_send, c_recv, *got,
):
    comps, width_x, width_y, depth = pops.shape
    fringe = prec.shape[1]
    turbines = loading.shape[1]
    blocks = width_y // BLOCK
    me, my = lax.axis_index("gx"), lax.axis_index("gy")
    right, left = lax.rem(me + 1, n), lax.rem(me + n - 1, n)
    above, below = lax.rem(my + 1, m), lax.rem(my + m - 1, m)

    prec_in = [
        pltpu.make_async_copy(prec_hbm.at[:, p], prec.at[:, p], in_sem.at[p]) for p in range(fringe)]
    small_in = [
        pltpu.make_async_copy(source, target, in_sem.at[fringe + 1 + k])
        for k, (source, target) in enumerate((
            (cols_hbm, cols), (turb_hbm, turb), (pairing_hbm, pairing), (rates_hbm, rates),
            (loading_hbm, loading)))]
    pops_in = pltpu.make_async_copy(pops_hbm, pops, in_sem.at[fringe])
    for copy in prec_in + small_in:
        copy.start()

    barrier = pltpu.get_barrier_semaphore()

    def greet_x(i, _):
        pl.semaphore_signal(barrier, inc=1, device_id={"gx": lax.rem(me + i, n)}, device_id_type=MESH)
        return 0

    def greet_y(i, _):
        pl.semaphore_signal(barrier, inc=1, device_id={"gy": lax.rem(my + i, m)}, device_id_type=MESH)
        return 0

    lax.fori_loop(1, n, greet_x, 0)
    lax.fori_loop(1, m, greet_y, 0)

    heights = lax.broadcasted_iota(jnp.int32, (BLOCK, depth), 1).astype(jnp.float32)
    profile = jnp.exp(-jnp.square((heights - depth / 3.0) / (depth / 6.0)))

    def span(j):
        return pl.ds(pl.multiple_of(j * chunk, BLOCK), chunk)

    def partner(i):
        return lax.rem(me + n // 2 + (i // 2) * (1 - 2 * lax.rem(i, 2)) + n, n)

    def first(p, i, sent):
        other = partner(i)
        slot = me if sent else other
        return pltpu.make_async_remote_copy(
            src_ref=mom.at[p, span(other), :], dst_ref=got[p].at[slot],
            send_sem=a_send.at[p * n + other], recv_sem=a_recv.at[p * n + slot],
            device_id={"gx": other}, device_id_type=MESH)

    def second(p, i, sent):
        other = partner(i)
        slot = me if sent else other
        return pltpu.make_async_remote_copy(
            src_ref=stage.at[p, other], dst_ref=final.at[p, span(slot), :],
            send_sem=b_send.at[p * n + other], recv_sem=b_recv.at[p * n + slot],
            device_id={"gx": other}, device_id_type=MESH)

    def total_x(i, sent):
        other = lax.rem(me + i, n)
        slot = me if sent else other
        return pltpu.make_async_remote_copy(
            src_ref=tot_x.at[slot], dst_ref=tot_x.at[slot],
            send_sem=tx_send.at[other], recv_sem=tx_recv.at[slot],
            device_id={"gx": other}, device_id_type=MESH)

    def total_y(i, sent):
        other = lax.rem(my + i, m)
        slot = my if sent else other
        return pltpu.make_async_remote_copy(
            src_ref=tot_y.at[slot], dst_ref=tot_y.at[slot],
            send_sem=ty_send.at[other], recv_sem=ty_recv.at[slot],
            device_id={"gy": other}, device_id_type=MESH)

    def each(count, action):
        def step(i, _):
            action(i)
            return 0

        lax.fori_loop(1, count, step, 0)

    for copy in prec_in:
        copy.wait()
    pops_in.start()
    for p in range(fringe):
        def precursor_block(b, _, p=p):
            rows = pl.ds(pl.multiple_of(b * BLOCK, BLOCK), BLOCK)
            moments = forward([prec[i, p, rows, :] for i in range(27)])
            for q in range(10):
                start = pl.multiple_of(q * width_y + b * BLOCK, BLOCK)
                mom[p, pl.ds(start, BLOCK), :] = moments[LOW[q]]
            return 0

        lax.fori_loop(0, blocks, precursor_block, 0)
        if p == 0:
            pl.semaphore_wait(barrier, n + m - 2)
        each(n, lambda i, p=p: first(p, i, True).start())

    for copy in small_in:
        copy.wait()
    slots = cols.shape[1]
    owner = (
        lax.broadcasted_iota(jnp.int32, (LANES, slots), 0) == turb[...]
    ).astype(jnp.float32).astype(jnp.bfloat16)
    contract = (((1,), (1,)), ((), ()))
    counts = lax.dot_general(
        jnp.ones((BLOCK, slots), jnp.bfloat16), owner, contract, preferred_element_type=jnp.float32)
    shape = (width_x, width_y, slots)
    column = (
        (lax.broadcasted_iota(jnp.int32, shape, 0) + me * width_x) * (width_y * m)
        + lax.broadcasted_iota(jnp.int32, shape, 1) + my * width_y)
    match = (column == cols[...].reshape(1, 1, slots)).astype(jnp.float32).astype(jnp.bfloat16)
    hits[...] = lax.dot_general(
        match.reshape(width_x * width_y, slots), owner, contract, preferred_element_type=jnp.float32
    ).reshape(width_x, width_y, LANES)

    pops_in.wait()

    def share(x, acc):
        sheets = []
        for kx in range(3):
            c = [pops[9 * kx + k, x] for k in range(9)]
            corner = (c[0] + c[2]) + (c[6] + c[8])
            edge = (c[1] + c[3]) + (c[5] + c[7])
            sheets.append(corner * (1.0 / 36.0) + edge * (1.0 / 9.0) + c[4] * (4.0 / 9.0))
        density = (sheets[0] + sheets[2]) * (1.0 / 6.0) + sheets[1] * (2.0 / 3.0)
        velocity = (sheets[2] - sheets[0]) * (1.0 / 6.0) / density
        return acc + jnp.sum(velocity * profile[:1], axis=1, keepdims=True) * hits[x]

    acc = lax.fori_loop(0, width_x, share, jnp.zeros((width_y, LANES), jnp.float32))
    tot_x[me] = jnp.sum(acc, axis=0, keepdims=True)
    each(n, lambda i: total_x(i, True).start())

    def collide_block(x, b):
        rows = pl.ds(pl.multiple_of(b * BLOCK, BLOCK), BLOCK)
        moments = forward([pops[i, x, rows, :] for i in range(27)])
        density = moments[0]
        inverse = 1.0 / density
        velocity = [moments[9] * inverse, moments[3] * inverse, moments[1] * inverse]
        balance = balance_moments(density, velocity)
        relaxed = []
        for i in range(27):
            gap = moments[i] if balance[i] is None else moments[i] - balance[i]
            relaxed.append(moments[i] - rates[i] * gap)
        for i, value in enumerate(backward(relaxed)):
            post[i, x + 1, rows, :] = value

    def collide(start, stop):
        def step(k, _):
            collide_block(k // blocks, k % blocks)
            return 0

        lax.fori_loop(start * blocks, stop * blocks, step, 0)

    def pass_on(p):
        got[p][me] = mom[p, span(me), :]
        each(n, lambda i: first(p, i, False).wait_recv())

        def forward_chunk(i, _):
            to = partner(i)
            stage[p, to] = got[p][pairing[to]]
            second(p, i, True).start()
            return 0

        lax.fori_loop(1, n, forward_chunk, 0)
        final[p, span(me), :] = got[p][pairing[me]]

    part = -(-width_x // (fringe + 1))
    for p in range(fringe):
        collide(p * part, (p + 1) * part)
        pass_on(p)

    each(n, lambda i: total_x(i, False).wait_recv())
    tot_y[my] = lax.fori_loop(1, n, lambda i, t: t + tot_x[i], tot_x[0])
    each(m, lambda i: total_y(i, True).start())
    collide(fringe * part, width_x)

    load_pad[...] = jnp.zeros((BLOCK, LANES), jnp.float32)
    load_pad[:, :turbines] = jnp.broadcast_to(loading[...], (BLOCK, turbines))
    norm = counts * jnp.sum(profile, axis=1, keepdims=True)
    each(m, lambda i: total_y(i, False).wait_recv())
    totals = lax.fori_loop(1, m, lambda i, t: t + tot_y[i], tot_y[0])
    disc_speed = totals / jnp.where(counts > 0.0, norm, 1.0)[:1]
    speed[...] = disc_speed[:, :turbines]
    thrust = 0.5 * load_pad[:1] * disc_speed * jnp.abs(disc_speed)

    def push(x, _):
        column = jnp.sum(hits[x] * thrust, axis=1, keepdims=True)
        kick = (-3.0 * column) * profile[:1]
        for i in range(9):
            post[i, x + 1] = post[i, x + 1] - kick
        for i in range(18, 27):
            post[i, x + 1] = post[i, x + 1] + kick
        return 0

    lax.fori_loop(0, width_x, push, 0)

    def x_copy(way):
        if way:
            src, dst, to = post.at[pl.ds(18, 9), width_x], post.at[pl.ds(18, 9), 0], right
        else:
            src, dst, to = post.at[pl.ds(0, 9), 1], post.at[pl.ds(0, 9), width_x + 1], left
        return pltpu.make_async_remote_copy(
            src_ref=src, dst_ref=dst, send_sem=x_send.at[way], recv_sem=x_recv.at[way],
            device_id={"gx": to}, device_id_type=MESH)

    def y_copy(way, late):
        planes = (late - 1, 1) if late else (fringe, width_x - fringe)
        return pltpu.make_async_remote_copy(
            src_ref=ysend.at[way, pl.ds(planes[0], planes[1])],
            dst_ref=yrecv.at[way, pl.ds(planes[0] + 1, planes[1])],
            send_sem=y_send.at[(fringe + 1) * way + late], recv_sem=y_recv.at[(fringe + 1) * way + late],
            device_id={"gy": above if way else below}, device_id_type=MESH)

    def corner_copy(way):
        if way:
            src, dst, to = yrecv.at[:, width_x, pl.ds(8, 8)], yrecv.at[:, 0, pl.ds(8, 8)], right
        else:
            src, dst, to = yrecv.at[:, 1, pl.ds(0, 8)], yrecv.at[:, width_x + 1, pl.ds(0, 8)], left
        return pltpu.make_async_remote_copy(
            src_ref=src, dst_ref=dst, send_sem=c_send.at[way], recv_sem=c_recv.at[way],
            device_id={"gx": to}, device_id_type=MESH)

    def pack(x, _):
        for way in range(2):
            edge = width_y - 1 if way else 0
            for kx in range(3):
                for kz in range(3):
                    row = row_of(kx, kz)
                    ysend[way, x, row : row + 1, :] = post[
                        9 * kx + 6 * way + kz, x + 1, edge : edge + 1, :]
        return 0

    lane = lax.broadcasted_iota(jnp.int32, (width_y, depth), 1)
    sub = lax.broadcasted_iota(jnp.int32, (width_y, depth), 0)

    def out_copy(x):
        return pltpu.make_async_copy(outv.at[:, x], out_hbm.at[:, x], out_sem.at[x])

    def stream(x, _):
        for i in range(27):
            kx, ky, kz = i // 9, (i // 3) % 3, i % 3
            source = x + 2 - kx
            moved = post[i, source]
            if ky != 1:
                way = 1 if ky == 2 else 0
                row = row_of(kx, kz)
                halo = yrecv[way, source, row : row + 1, :]
                moved = pltpu.roll(moved, 1 if way else width_y - 1, 0)
                moved = jnp.where(sub == (0 if way else width_y - 1), halo, moved)
            if kz != 1:
                moved = pltpu.roll(moved, 1 if kz == 2 else depth - 1, 1)
                moved = jnp.where(lane == (0 if kz == 2 else depth - 1), post[26 - i, x + 1], moved)
            outv[i, x] = moved
        out_copy(x).start()
        return 0

    x_copy(1).start()
    lax.fori_loop(fringe, width_x, pack, 0)
    for way in range(2):
        y_copy(way, 0).start()

    for p in range(fringe):
        blend = 0.5 / (p + 1.0)
        each(n, lambda i, p=p: second(p, i, False).wait_recv())

        def blend_block(b, _, p=p, blend=blend):
            rows = pl.ds(pl.multiple_of(b * BLOCK, BLOCK), BLOCK)
            low = []
            for q in range(10):
                start = pl.multiple_of(q * width_y + b * BLOCK, BLOCK)
                low.append(final[p, pl.ds(start, BLOCK), :])
            for i, value in enumerate(rebuild(low)):
                post[i, p + 1, rows, :] = (1.0 - blend) * post[i, p + 1, rows, :] + blend * value
            return 0

        lax.fori_loop(0, blocks, blend_block, 0)
        if p == 0:
            x_copy(0).start()
        pack(p, 0)
        for way in range(2):
            y_copy(way, p + 1).start()
        if p == 0:
            for way in range(2):
                y_copy(way, 0).wait_recv()
            corner_copy(1).start()
            lax.fori_loop(fringe + 1, width_x - 1, stream, 0)
            for way in range(2):
                y_copy(way, 1).wait_recv()
            corner_copy(0).start()

    for late in range(2, fringe + 1):
        for way in range(2):
            y_copy(way, late).wait_recv()
    x_copy(1).wait_recv()
    corner_copy(1).wait_recv()
    lax.fori_loop(0, fringe + 1, stream, 0)
    x_copy(0).wait_recv()
    corner_copy(0).wait_recv()
    lax.fori_loop(width_x - 1, width_x, stream, 0)

    for p in range(fringe):
        each(n, lambda i, p=p: first(p, i, True).wait_send())
        each(n, lambda i, p=p: second(p, i, True).wait_send())
    each(n, lambda i: total_x(i, True).wait_send())
    each(m, lambda i: total_y(i, True).wait_send())
    for way in range(2):
        x_copy(way).wait_send()
        corner_copy(way).wait_send()
        for late in range(fringe + 1):
            y_copy(way, late).wait_send()

    def drain(x, _):
        out_copy(x).wait()
        return 0

    lax.fori_loop(0, width_x, drain, 0)


def deliver_kernel(out_from, speed_from, out_to, speed_to, sems):
    count = out_from.shape[0]

    def copy(i):
        return pltpu.make_async_copy(out_from.at[i], out_to.at[i], sems.at[i])

    copies = [copy(i) for i in range(count)]
    copies.append(pltpu.make_async_copy(speed_from, speed_to, sems.at[count]))
    for item in copies:
        item.start()
    for item in copies:
        item.wait()


def deliver(out, speed, turbines):
    anywhere = pl.BlockSpec(memory_space=pl.ANY)
    vmem = pltpu.VMEM
    out, speed = pl.pallas_call(
        deliver_kernel,
        out_shape=(pltpu.HBM(out.shape, out.dtype), pltpu.HBM(speed.shape, speed.dtype)),
        in_specs=[anywhere, anywhere],
        out_specs=(anywhere, anywhere),
        scratch_shapes=[pltpu.SemaphoreType.DMA((out.shape[0] + 1,))],
    )(pltpu.with_memory_space_constraint(out, vmem), pltpu.with_memory_space_constraint(speed, vmem))
    return out, speed.reshape(turbines)


def body(n, m, populations, precursor, pairing, rates, loading, disc_cols, disc_turb):
    comps, width_x, width_y, depth = populations.shape
    fringe = precursor.shape[1]
    rows = 10 * width_y
    chunk = -(-rows // (n * BLOCK)) * BLOCK
    turbines = loading.shape[0]
    slots = disc_cols.shape[0]
    f32 = jnp.float32
    anywhere = pl.BlockSpec(memory_space=pl.ANY)
    hbm = pl.BlockSpec(memory_space=pltpu.HBM)
    vmem = pl.BlockSpec(memory_space=pltpu.VMEM)
    dma = pltpu.SemaphoreType.DMA
    out, speed = pl.pallas_call(
        functools.partial(kernel, n, m, chunk),
        out_shape=(
            pltpu.VMEM(populations.shape, f32),
            pltpu.VMEM((1, turbines), f32),
        ),
        in_specs=[hbm] * 7,
        out_specs=(anywhere, vmem),
        scratch_shapes=[
            pltpu.VMEM(populations.shape, f32),
            pltpu.VMEM(precursor.shape, f32),
            pltpu.SMEM(pairing.shape, jnp.int32),
            pltpu.SMEM(rates.shape, f32),
            pltpu.VMEM((1, turbines), f32),
            pltpu.VMEM((1, slots), jnp.int32),
            pltpu.VMEM((1, slots), jnp.int32),
            pltpu.VMEM((comps, width_x + 2, width_y, depth), f32),
            pltpu.VMEM(populations.shape, f32),
            pltpu.VMEM((fringe, n * chunk, depth), f32),
            pltpu.VMEM((fringe, n, chunk, depth), f32),
            pltpu.VMEM((fringe, n * chunk, depth), f32),
            pltpu.VMEM((n, 1, LANES), f32),
            pltpu.VMEM((m, 1, LANES), f32),
            pltpu.VMEM((BLOCK, LANES), f32),
            pltpu.VMEM((width_x, width_y, LANES), f32),
            pltpu.VMEM((2, width_x, 16, depth), f32),
            pltpu.VMEM((2, width_x + 2, 16, depth), f32),
            dma((fringe + 6,)), dma((width_x,)),
            dma((fringe * n,)), dma((fringe * n,)), dma((fringe * n,)), dma((fringe * n,)),
            dma((n,)), dma((n,)), dma((m,)), dma((m,)),
            dma((2,)), dma((2,)), dma((2 * fringe + 2,)), dma((2 * fringe + 2,)), dma((2,)), dma((2,)),
        ] + [pltpu.VMEM((n, chunk, depth), f32)] * fringe,
        compiler_params=pltpu.CompilerParams(
            collective_id=0, has_side_effects=True, vmem_limit_bytes=40 * 1024 * 1024),
    )(*(pltpu.with_memory_space_constraint(x, pltpu.HBM) for x in (
        populations, precursor, pairing, rates,
        loading.reshape(1, turbines), disc_cols.reshape(1, slots), disc_turb.reshape(1, slots),
    )))
    return deliver(out, speed, turbines)


def solution(mesh):
    n, m = mesh.shape["gx"], mesh.shape["gy"]
    in_specs = (P(None, "gx", "gy", None), P(None, "gx", "gy", None), P(), P(), P(), P(), P())
    out_specs = (P(None, "gx", "gy", None), P())
    return jax.shard_map(
        functools.partial(body, n, m), mesh=mesh, in_specs=in_specs, out_specs=out_specs, check_vma=False)
```

```python
import functools
import jax
import jax.numpy as jnp
import numpy as np
from jax import lax
from jax.experimental import pallas as pl
from jax.experimental.pallas import tpu as pltpu
from jax.sharding import PartitionSpec as P

MESH = pl.DeviceIdType.MESH
LANES = 128
BLOCK = 8
LOW = (0, 9, 3, 1, 18, 6, 2, 12, 10, 4)


def forward(cells):
    cells = list(cells)
    for stride in (9, 3, 1):
        for i in range(27):
            if (i // stride) % 3 == 0:
                low, mid, high = cells[i], cells[i + stride], cells[i + 2 * stride]
                even = (low + high) * (1.0 / 6.0)
                cells[i] = even + mid * (2.0 / 3.0)
                cells[i + stride] = (high - low) * (1.0 / 6.0)
                cells[i + 2 * stride] = even
    return cells


def backward(moments):
    cells = list(moments)
    for stride in (9, 3, 1):
        for i in range(27):
            if (i // stride) % 3 == 0:
                zero, one, two = cells[i], cells[i + stride], cells[i + 2 * stride]
                odd, even = one * 3.0, two * 3.0
                cells[i] = even - odd
                cells[i + stride] = (zero - two) * 1.5
                cells[i + 2 * stride] = even + odd
    return cells


def balance_moments(density, velocity):
    flux = [density * v for v in velocity]
    out = []
    for i in range(27):
        powers = (i // 9, (i // 3) % 3, i % 3)
        scale = (1.0 / 3.0) ** sum(p == 2 for p in powers)
        odd = [d for d in range(3) if powers[d] == 1]
        if len(odd) == 3:
            out.append(None)
            continue
        if len(odd) == 2:
            value = flux[odd[0]] * velocity[odd[1]]
        elif len(odd) == 1:
            value = flux[odd[0]]
        else:
            value = density
            for d in range(3):
                if powers[d] == 2:
                    value = value + 3.0 * (flux[d] * velocity[d])
        out.append(value if scale == 1.0 else value * scale)
    return out


def rebuild(low):
    rho, jx, jy, jz, xx, yy, zz, xy, xz, yz = low
    base = 2.5 * rho - 1.5 * (xx + yy + zz)
    third = rho * (1.0 / 3.0)
    linear = (3.0 * jx, 3.0 * jy, 3.0 * jz)
    square = (4.5 * (xx - third), 4.5 * (yy - third), 4.5 * (zz - third))
    cross = (9.0 * xy, 9.0 * xz, 9.0 * yz)

    def one(d, step):
        return square[d] + linear[d] if step > 0 else square[d] - linear[d]

    def signed(value, term, sign):
        return value + term if sign > 0 else value - term

    out = []
    for i in range(27):
        steps = (i // 9 - 1, (i // 3) % 3 - 1, i % 3 - 1)
        value = base
        for d in range(3):
            if steps[d]:
                value = value + one(d, steps[d])
        for (a, b), term in zip(((0, 1), (0, 2), (1, 2)), cross):
            if steps[a] * steps[b]:
                value = signed(value, term, steps[a] * steps[b])
        out.append(value)
    return out


def row_of(kx, kz):
    return kx * 3 + kz if kx < 2 else 8 + kz


def kernel(
    n, m, chunk,
    pops_hbm, prec_hbm, pairing_hbm, rates_hbm, loading_hbm, cols_hbm, turb_hbm,
    out_hbm, speed,
    pops, prec, pairing, rates, loading, cols, turb,
    post, outv, mom, stage, final, tot_x, tot_y, load_pad, hits, ysend, yrecv,
    in_sem, out_sem, a_send, a_recv, b_send, b_recv, tx_send, tx_recv, ty_send, ty_recv,
    x_send, x_recv, y_send, y_recv, c_send, c_recv, *got,
):
    comps, width_x, width_y, depth = pops.shape
    fringe = prec.shape[1]
    turbines = loading.shape[1]
    blocks = width_y // BLOCK
    me, my = lax.axis_index("gx"), lax.axis_index("gy")
    right, left = lax.rem(me + 1, n), lax.rem(me + n - 1, n)
    above, below = lax.rem(my + 1, m), lax.rem(my + m - 1, m)

    prec_in = [
        pltpu.make_async_copy(prec_hbm.at[:, p], prec.at[:, p], in_sem.at[p]) for p in range(fringe)]
    small_in = [
        pltpu.make_async_copy(source, target, in_sem.at[fringe + 1 + k])
        for k, (source, target) in enumerate((
            (cols_hbm, cols), (turb_hbm, turb), (pairing_hbm, pairing), (rates_hbm, rates),
            (loading_hbm, loading)))]
    pops_in = pltpu.make_async_copy(pops_hbm, pops, in_sem.at[fringe])
    for copy in prec_in + small_in + [pops_in]:
        copy.start()

    barrier = pltpu.get_barrier_semaphore()

    def greet_x(i, _):
        pl.semaphore_signal(barrier, inc=1, device_id={"gx": lax.rem(me + i, n)}, device_id_type=MESH)
        return 0

    def greet_y(i, _):
        pl.semaphore_signal(barrier, inc=1, device_id={"gy": lax.rem(my + i, m)}, device_id_type=MESH)
        return 0

    lax.fori_loop(1, n, greet_x, 0)
    lax.fori_loop(1, m, greet_y, 0)

    heights = lax.broadcasted_iota(jnp.int32, (BLOCK, depth), 1).astype(jnp.float32)
    profile = jnp.exp(-jnp.square((heights - depth / 3.0) / (depth / 6.0)))

    def span(j):
        return pl.ds(pl.multiple_of(j * chunk, BLOCK), chunk)

    def first(p, i, sent):
        other = lax.rem(me + i, n)
        slot = me if sent else other
        return pltpu.make_async_remote_copy(
            src_ref=mom.at[p, span(other), :], dst_ref=got[p].at[slot],
            send_sem=a_send.at[p * n + other], recv_sem=a_recv.at[p * n + slot],
            device_id={"gx": other}, device_id_type=MESH)

    def second(p, i, sent):
        other = lax.rem(me + i, n)
        slot = me if sent else other
        return pltpu.make_async_remote_copy(
            src_ref=stage.at[p, other], dst_ref=final.at[p, span(slot), :],
            send_sem=b_send.at[p * n + other], recv_sem=b_recv.at[p * n + slot],
            device_id={"gx": other}, device_id_type=MESH)

    def total_x(i, sent):
        other = lax.rem(me + i, n)
        slot = me if sent else other
        return pltpu.make_async_remote_copy(
            src_ref=tot_x.at[slot], dst_ref=tot_x.at[slot],
            send_sem=tx_send.at[other], recv_sem=tx_recv.at[slot],
            device_id={"gx": other}, device_id_type=MESH)

    def total_y(i, sent):
        other = lax.rem(my + i, m)
        slot = my if sent else other
        return pltpu.make_async_remote_copy(
            src_ref=tot_y.at[slot], dst_ref=tot_y.at[slot],
            send_sem=ty_send.at[other], recv_sem=ty_recv.at[slot],
            device_id={"gy": other}, device_id_type=MESH)

    def each(count, action):
        def step(i, _):
            action(i)
            return 0

        lax.fori_loop(1, count, step, 0)

    for p in range(fringe):
        prec_in[p].wait()

        def precursor_block(b, _, p=p):
            rows = pl.ds(pl.multiple_of(b * BLOCK, BLOCK), BLOCK)
            moments = forward([prec[i, p, rows, :] for i in range(27)])
            for q in range(10):
                start = pl.multiple_of(q * width_y + b * BLOCK, BLOCK)
                mom[p, pl.ds(start, BLOCK), :] = moments[LOW[q]]
            return 0

        lax.fori_loop(0, blocks, precursor_block, 0)
        if p == 0:
            pl.semaphore_wait(barrier, n + m - 2)
        each(n, lambda i, p=p: first(p, i, True).start())

    for copy in small_in:
        copy.wait()
    slots = cols.shape[1]
    owner = (
        lax.broadcasted_iota(jnp.int32, (LANES, slots), 0) == turb[...]
    ).astype(jnp.float32).astype(jnp.bfloat16)
    contract = (((1,), (1,)), ((), ()))
    counts = lax.dot_general(
        jnp.ones((BLOCK, slots), jnp.bfloat16), owner, contract, preferred_element_type=jnp.float32)
    shape = (width_x, width_y, slots)
    column = (
        (lax.broadcasted_iota(jnp.int32, shape, 0) + me * width_x) * (width_y * m)
        + lax.broadcasted_iota(jnp.int32, shape, 1) + my * width_y)
    match = (column == cols[...].reshape(1, 1, slots)).astype(jnp.float32).astype(jnp.bfloat16)
    hits[...] = lax.dot_general(
        match.reshape(width_x * width_y, slots), owner, contract, preferred_element_type=jnp.float32
    ).reshape(width_x, width_y, LANES)

    pops_in.wait()

    def share(x, acc):
        sheets = []
        for kx in range(3):
            c = [pops[9 * kx + k, x] for k in range(9)]
            corner = (c[0] + c[2]) + (c[6] + c[8])
            edge = (c[1] + c[3]) + (c[5] + c[7])
            sheets.append(corner * (1.0 / 36.0) + edge * (1.0 / 9.0) + c[4] * (4.0 / 9.0))
        density = (sheets[0] + sheets[2]) * (1.0 / 6.0) + sheets[1] * (2.0 / 3.0)
        velocity = (sheets[2] - sheets[0]) * (1.0 / 6.0) / density
        return acc + jnp.sum(velocity * profile[:1], axis=1, keepdims=True) * hits[x]

    acc = lax.fori_loop(0, width_x, share, jnp.zeros((width_y, LANES), jnp.float32))
    tot_x[me] = jnp.sum(acc, axis=0, keepdims=True)
    each(n, lambda i: total_x(i, True).start())

    def collide_block(x, b):
        rows = pl.ds(pl.multiple_of(b * BLOCK, BLOCK), BLOCK)
        moments = forward([pops[i, x, rows, :] for i in range(27)])
        density = moments[0]
        inverse = 1.0 / density
        velocity = [moments[9] * inverse, moments[3] * inverse, moments[1] * inverse]
        balance = balance_moments(density, velocity)
        relaxed = []
        for i in range(27):
            gap = moments[i] if balance[i] is None else moments[i] - balance[i]
            relaxed.append(moments[i] - rates[i] * gap)
        for i, value in enumerate(backward(relaxed)):
            post[i, x + 1, rows, :] = value

    def collide(start, stop):
        def step(k, _):
            collide_block(k // blocks, k % blocks)
            return 0

        lax.fori_loop(start * blocks, stop * blocks, step, 0)

    def pass_on(p):
        got[p][me] = mom[p, span(me), :]
        each(n, lambda i: first(p, i, False).wait_recv())

        def forward_chunk(i, _):
            to = lax.rem(me + i, n)
            stage[p, to] = got[p][pairing[to]]
            second(p, i, True).start()
            return 0

        lax.fori_loop(1, n, forward_chunk, 0)
        final[p, span(me), :] = got[p][pairing[me]]

    part = -(-width_x // (fringe + 1))
    for p in range(fringe):
        if p:
            collide((p - 1) * part, p * part)
        pass_on(p)

    each(n, lambda i: total_x(i, False).wait_recv())
    tot_y[my] = lax.fori_loop(1, n, lambda i, t: t + tot_x[i], tot_x[0])
    each(m, lambda i: total_y(i, True).start())
    collide((fringe - 1) * part, width_x)

    load_pad[...] = jnp.zeros((BLOCK, LANES), jnp.float32)
    load_pad[:, :turbines] = jnp.broadcast_to(loading[...], (BLOCK, turbines))
    norm = counts * jnp.sum(profile, axis=1, keepdims=True)
    each(m, lambda i: total_y(i, False).wait_recv())
    totals = lax.fori_loop(1, m, lambda i, t: t + tot_y[i], tot_y[0])
    disc_speed = totals / jnp.where(counts > 0.0, norm, 1.0)[:1]
    speed[...] = disc_speed[:, :turbines]
    thrust = 0.5 * load_pad[:1] * disc_speed * jnp.abs(disc_speed)

    def push(x, _):
        column = jnp.sum(hits[x] * thrust, axis=1, keepdims=True)
        kick = (-3.0 * column) * profile[:1]
        for i in range(9):
            post[i, x + 1] = post[i, x + 1] - kick
        for i in range(18, 27):
            post[i, x + 1] = post[i, x + 1] + kick
        return 0

    lax.fori_loop(0, width_x, push, 0)

    def x_copy(way):
        if way:
            src, dst, to = post.at[pl.ds(18, 9), width_x], post.at[pl.ds(18, 9), 0], right
        else:
            src, dst, to = post.at[pl.ds(0, 9), 1], post.at[pl.ds(0, 9), width_x + 1], left
        return pltpu.make_async_remote_copy(
            src_ref=src, dst_ref=dst, send_sem=x_send.at[way], recv_sem=x_recv.at[way],
            device_id={"gx": to}, device_id_type=MESH)

    def y_copy(way, late):
        planes = (late - 1, 1) if late else (fringe, width_x - fringe)
        return pltpu.make_async_remote_copy(
            src_ref=ysend.at[way, pl.ds(planes[0], planes[1])],
            dst_ref=yrecv.at[way, pl.ds(planes[0] + 1, planes[1])],
            send_sem=y_send.at[(fringe + 1) * way + late], recv_sem=y_recv.at[(fringe + 1) * way + late],
            device_id={"gy": above if way else below}, device_id_type=MESH)

    def corner_copy(way):
        if way:
            src, dst, to = yrecv.at[:, width_x, pl.ds(8, 8)], yrecv.at[:, 0, pl.ds(8, 8)], right
        else:
            src, dst, to = yrecv.at[:, 1, pl.ds(0, 8)], yrecv.at[:, width_x + 1, pl.ds(0, 8)], left
        return pltpu.make_async_remote_copy(
            src_ref=src, dst_ref=dst, send_sem=c_send.at[way], recv_sem=c_recv.at[way],
            device_id={"gx": to}, device_id_type=MESH)

    def pack(x, _):
        for way in range(2):
            edge = width_y - 1 if way else 0
            for kx in range(3):
                for kz in range(3):
                    row = row_of(kx, kz)
                    ysend[way, x, row : row + 1, :] = post[
                        9 * kx + 6 * way + kz, x + 1, edge : edge + 1, :]
        return 0

    lane = lax.broadcasted_iota(jnp.int32, (width_y, depth), 1)
    sub = lax.broadcasted_iota(jnp.int32, (width_y, depth), 0)

    def out_copy(x):
        return pltpu.make_async_copy(outv.at[:, x], out_hbm.at[:, x], out_sem.at[x])

    def stream(x, _):
        for i in range(27):
            kx, ky, kz = i // 9, (i // 3) % 3, i % 3
            source = x + 2 - kx
            moved = post[i, source]
            if ky != 1:
                way = 1 if ky == 2 else 0
                row = row_of(kx, kz)
                halo = yrecv[way, source, row : row + 1, :]
                moved = pltpu.roll(moved, 1 if way else width_y - 1, 0)
                moved = jnp.where(sub == (0 if way else width_y - 1), halo, moved)
            if kz != 1:
                moved = pltpu.roll(moved, 1 if kz == 2 else depth - 1, 1)
                moved = jnp.where(lane == (0 if kz == 2 else depth - 1), post[26 - i, x + 1], moved)
            outv[i, x] = moved
        out_copy(x).start()
        return 0

    x_copy(1).start()
    lax.fori_loop(fringe, width_x, pack, 0)
    for way in range(2):
        y_copy(way, 0).start()

    for p in range(fringe):
        blend = 0.5 / (p + 1.0)
        each(n, lambda i, p=p: second(p, i, False).wait_recv())

        def blend_block(b, _, p=p, blend=blend):
            rows = pl.ds(pl.multiple_of(b * BLOCK, BLOCK), BLOCK)
            low = []
            for q in range(10):
                start = pl.multiple_of(q * width_y + b * BLOCK, BLOCK)
                low.append(final[p, pl.ds(start, BLOCK), :])
            for i, value in enumerate(rebuild(low)):
                post[i, p + 1, rows, :] = (1.0 - blend) * post[i, p + 1, rows, :] + blend * value
            return 0

        lax.fori_loop(0, blocks, blend_block, 0)
        if p == 0:
            x_copy(0).start()
        pack(p, 0)
        for way in range(2):
            y_copy(way, p + 1).start()
        if p == 0:
            for way in range(2):
                y_copy(way, 0).wait_recv()
            corner_copy(1).start()
            lax.fori_loop(fringe + 1, width_x - 1, stream, 0)
            for way in range(2):
                y_copy(way, 1).wait_recv()
            corner_copy(0).start()

    for late in range(2, fringe + 1):
        for way in range(2):
            y_copy(way, late).wait_recv()
    x_copy(1).wait_recv()
    corner_copy(1).wait_recv()
    lax.fori_loop(0, fringe + 1, stream, 0)
    x_copy(0).wait_recv()
    corner_copy(0).wait_recv()
    lax.fori_loop(width_x - 1, width_x, stream, 0)

    for p in range(fringe):
        each(n, lambda i, p=p: first(p, i, True).wait_send())
        each(n, lambda i, p=p: second(p, i, True).wait_send())
    each(n, lambda i: total_x(i, True).wait_send())
    each(m, lambda i: total_y(i, True).wait_send())
    for way in range(2):
        x_copy(way).wait_send()
        corner_copy(way).wait_send()
        for late in range(fringe + 1):
            y_copy(way, late).wait_send()

    def drain(x, _):
        out_copy(x).wait()
        return 0

    lax.fori_loop(0, width_x, drain, 0)


def deliver_kernel(out_from, speed_from, out_to, speed_to, sems):
    count = out_from.shape[0]

    def copy(i):
        return pltpu.make_async_copy(out_from.at[i], out_to.at[i], sems.at[i])

    copies = [copy(i) for i in range(count)]
    copies.append(pltpu.make_async_copy(speed_from, speed_to, sems.at[count]))
    for item in copies:
        item.start()
    for item in copies:
        item.wait()


def deliver(out, speed, turbines):
    anywhere = pl.BlockSpec(memory_space=pl.ANY)
    vmem = pltpu.VMEM
    out, speed = pl.pallas_call(
        deliver_kernel,
        out_shape=(pltpu.HBM(out.shape, out.dtype), pltpu.HBM(speed.shape, speed.dtype)),
        in_specs=[anywhere, anywhere],
        out_specs=(anywhere, anywhere),
        scratch_shapes=[pltpu.SemaphoreType.DMA((out.shape[0] + 1,))],
    )(pltpu.with_memory_space_constraint(out, vmem), pltpu.with_memory_space_constraint(speed, vmem))
    return out, speed.reshape(turbines)


def body(n, m, populations, precursor, pairing, rates, loading, disc_cols, disc_turb):
    comps, width_x, width_y, depth = populations.shape
    fringe = precursor.shape[1]
    rows = 10 * width_y
    chunk = -(-rows // (n * BLOCK)) * BLOCK
    turbines = loading.shape[0]
    slots = disc_cols.shape[0]
    f32 = jnp.float32
    anywhere = pl.BlockSpec(memory_space=pl.ANY)
    hbm = pl.BlockSpec(memory_space=pltpu.HBM)
    vmem = pl.BlockSpec(memory_space=pltpu.VMEM)
    dma = pltpu.SemaphoreType.DMA
    out, speed = pl.pallas_call(
        functools.partial(kernel, n, m, chunk),
        out_shape=(
            pltpu.VMEM(populations.shape, f32),
            pltpu.VMEM((1, turbines), f32),
        ),
        in_specs=[hbm] * 7,
        out_specs=(anywhere, vmem),
        scratch_shapes=[
            pltpu.VMEM(populations.shape, f32),
            pltpu.VMEM(precursor.shape, f32),
            pltpu.SMEM(pairing.shape, jnp.int32),
            pltpu.SMEM(rates.shape, f32),
            pltpu.VMEM((1, turbines), f32),
            pltpu.VMEM((1, slots), jnp.int32),
            pltpu.VMEM((1, slots), jnp.int32),
            pltpu.VMEM((comps, width_x + 2, width_y, depth), f32),
            pltpu.VMEM(populations.shape, f32),
            pltpu.VMEM((fringe, n * chunk, depth), f32),
            pltpu.VMEM((fringe, n, chunk, depth), f32),
            pltpu.VMEM((fringe, n * chunk, depth), f32),
            pltpu.VMEM((n, 1, LANES), f32),
            pltpu.VMEM((m, 1, LANES), f32),
            pltpu.VMEM((BLOCK, LANES), f32),
            pltpu.VMEM((width_x, width_y, LANES), f32),
            pltpu.VMEM((2, width_x, 16, depth), f32),
            pltpu.VMEM((2, width_x + 2, 16, depth), f32),
            dma((fringe + 6,)), dma((width_x,)),
            dma((fringe * n,)), dma((fringe * n,)), dma((fringe * n,)), dma((fringe * n,)),
            dma((n,)), dma((n,)), dma((m,)), dma((m,)),
            dma((2,)), dma((2,)), dma((2 * fringe + 2,)), dma((2 * fringe + 2,)), dma((2,)), dma((2,)),
        ] + [pltpu.VMEM((n, chunk, depth), f32)] * fringe,
        compiler_params=pltpu.CompilerParams(
            collective_id=0, has_side_effects=True, vmem_limit_bytes=40 * 1024 * 1024),
    )(*(pltpu.with_memory_space_constraint(x, pltpu.HBM) for x in (
        populations, precursor, pairing, rates,
        loading.reshape(1, turbines), disc_cols.reshape(1, slots), disc_turb.reshape(1, slots),
    )))
    return deliver(out, speed, turbines)


def solution(mesh):
    n, m = mesh.shape["gx"], mesh.shape["gy"]
    in_specs = (P(None, "gx", "gy", None), P(None, "gx", "gy", None), P(), P(), P(), P(), P())
    out_specs = (P(None, "gx", "gy", None), P())
    return jax.shard_map(
        functools.partial(body, n, m), mesh=mesh, in_specs=in_specs, out_specs=out_specs, check_vma=False)
```
